32 devices in a mesh: fsdp: 4 (over y, core), ctx: 8 (over z, x).
Axes of the slice: x: 2, y: 2, z: 4, core: 2. Of those that a mesh axis runs over, the one named last changes fastest.
Arguments:
- tokens: bfloat16 [4, 1024, 4096], P('fsdp', 'ctx'), may hold values from -6 to 6
- segments: int32 [4, 1024], P(None, 'ctx'), may hold values from 0 to 7, never falling along the last dimension, each value on 1 to 512 neighbouring positions
- gate_weight: bfloat16 [4096, 4096], P(None, 'fsdp'), may hold values from -0.09375 to 0.09375
- value_weight: bfloat16 [4096, 4096], P(None, 'fsdp'), may hold values from -0.09375 to 0.09375
- coupling_weight: bfloat16 [4096, 2048], P(None, 'fsdp'), may hold values from -0.09375 to 0.09375
- step_weight: bfloat16 [4096, 64], P(None, 'fsdp'), may hold values from -0.09375 to 0.09375
- value_conv: bfloat16 [4, 4096], P(None, 'fsdp'), may hold values from -3 to 3
- coupling_conv: bfloat16 [4, 2048], P(None, 'fsdp'), may hold values from -3 to 3
- value_shift: float32 [4096], P('fsdp'), may hold values from -3 to 3
- coupling_shift: float32 [2048], P('fsdp'), may hold values from -3 to 3
- step_bias: float32 [64], P('fsdp'), may hold values from -4.5 to -1.5
- decay_log: float32 [64], P('fsdp'), may hold values from -4.6 to 2.3
- skip_gain: float32 [64], P('fsdp'), may hold values from 0.5 to 1.5
- norm_gain: float32 [4096], P('fsdp'), may hold values from 0.1 to 1.9
- out_weight: bfloat16 [4096, 4096], P('fsdp'), may hold values from -0.09375 to 0.09375
- rezero: float32 [1], replicated, may hold values from 0.5 to 1.5
Outputs:
- mixed: bfloat16 [4, 1024, 4096], P('fsdp', 'ctx')
The draws below stay inside these ranges and needn't reach their ends.
Inputs may be any that keep to these rules, and one draw needn't show every extreme that they name: `segments`: along each stream the ids never fall; every document has 1 to 512 tokens and one of them exactly 512.
All inputs are finite; a program needn't handle non-finite values.
Results may differ from the reference program's by a relative error of at most 0.0064.
Values may be sent and summed in bfloat16 or wider, within the bound.
No kernel may reach another device: no remote copies, remote signals or barrier semaphores. Data moves between devices by JAX's collectives and lax.ppermute only.
A program may use at most 128 MiB of HBM per device.

```python
import math
import jax
import jax.numpy as jnp
import numpy as np
from jax import lax

D = 4096
H = 64
P_SIZE = 64
N = 128
G = 8
CH = 128
K = 4
LEN = 1024
STREAMS = 4


def level_of(stream_key, extent, cuts, least, high):
    loudness, own = 1.0, jax.random.fold_in(stream_key, 6)
    for dim, blocks in cuts:
        steps = jnp.exp(jax.random.uniform(jax.random.fold_in(own, dim), (blocks,), jnp.float32, least / len(cuts), high / len(cuts)))
        loudness = loudness * jnp.repeat(steps, extent[dim] // blocks).reshape([-1 if axis == dim else 1 for axis in range(len(extent))])
    return loudness


def profile(amount, total, bound, slope):
    portions = [(1 << 20) // math.isqrt(standing ** slope) + 1 for standing in range(2, amount + 1)]
    spare, counts = total - bound - (amount - 1), [1] * (amount - 1)
    while spare > 0:
        free = [i for i in range(amount - 1) if counts[i] < bound]
        whole, budget = sum([portions[i] for i in free]), spare
        for i in free:
            addition = min(bound - counts[i], max(1, budget * portions[i] // whole), spare)
            counts[i] = counts[i] + addition
            spare = spare - addition
    return np.array([bound] + counts)


def ragged_sizes(key, number_of, total, bound, lean):
    if number_of == 2:
        one = jax.random.randint(key, (), max(1, total - bound), min(bound, total - 1) + 1)
        return jnp.stack([one, total - one])
    sizes = jnp.asarray(profile(number_of, total, bound, lean), jnp.int32)
    pairs = (number_of - 1) // 2
    source_of, sink = sizes[1:1 + 2 * pairs:2], sizes[2:2 + 2 * pairs:2]
    slack = jnp.minimum(source_of - 1, bound - sink)
    passed = jax.random.randint(jax.random.fold_in(key, 1), (pairs,), 0, 1 << 20) % (slack + 1)
    sizes = sizes.at[1:1 + 2 * pairs:2].set(source_of - passed).at[2:2 + 2 * pairs:2].set(sink + passed)
    return sizes[jax.random.permutation(jax.random.fold_in(key, 2), number_of)]


def centred(rng, extent, scale, bound, pieces=(), kind=jnp.bfloat16):
    factor_of = level_of(rng, extent, pieces, -0.22, 0.18) if pieces else 1.0
    entries = jax.random.normal(rng, extent, jnp.float32) * scale * factor_of
    return jnp.minimum(jnp.maximum(entries, -bound), bound).astype(kind)


def setup_inputs(seed: int = 0) -> dict:
    seeds = jax.random.split(jax.random.key(seed), 17)
    tokens = centred(seeds[0], (STREAMS, LEN, D), 1.0, 6.0, ((0, 4), (1, 8)))
    segments = jax.vmap(lambda own: jnp.searchsorted(jnp.cumsum(ragged_sizes(own, 8, LEN, LEN // 2, 2)), jnp.arange(LEN), side="right"))(jax.random.split(seeds[1], STREAMS)).reshape((STREAMS, LEN)).astype(jnp.int32)
    gate_weight = centred(seeds[2], (D, H * P_SIZE), D ** -0.5, 0.09375, ((1, 4),))
    value_weight = centred(seeds[3], (D, H * P_SIZE), D ** -0.5, 0.09375, ((1, 4),))
    coupling_weight = centred(seeds[4], (D, 2 * G * N), D ** -0.5, 0.09375, ((1, 4),))
    step_weight = centred(seeds[5], (D, H), D ** -0.5, 0.09375, ((1, 4),))
    value_conv = centred(seeds[6], (K, H * P_SIZE), K ** -0.5, 3.0, ((1, 4),))
    coupling_conv = centred(seeds[7], (K, 2 * G * N), K ** -0.5, 3.0, ((1, 4),))
    value_shift = centred(seeds[8], (H * P_SIZE,), 0.5, 3.0, ((0, 4),), jnp.float32)
    coupling_shift = centred(seeds[9], (2 * G * N,), 0.5, 3.0, ((0, 4),), jnp.float32)
    step_bias = jnp.clip(-4.5 + 3.0 * jax.random.uniform(seeds[10], (H,), jnp.float32) ** level_of(seeds[10], (H,), ((0, 4),), -0.2, 0.2), -4.5, -1.5)
    decay_log = jnp.clip(-4.6 + 6.8999998569488525 * jax.random.uniform(seeds[11], (H,), jnp.float32) ** level_of(seeds[11], (H,), ((0, 4),), -0.2, 0.2), -4.6, 2.3)
    skip_gain = jnp.clip(0.5 + 1.0 * jax.random.uniform(seeds[12], (H,), jnp.float32) ** level_of(seeds[12], (H,), ((0, 4),), -0.2, 0.2), 0.5, 1.5)
    norm_gain = jnp.clip(1.0 + 0.18 * jax.random.normal(seeds[13], (H * P_SIZE,), jnp.float32), 0.1, 1.9)
    out_weight = centred(seeds[14], (H * P_SIZE, D), (H * P_SIZE) ** -0.5, 0.09375, ((0, 4),))
    rezero = jnp.clip(jax.random.uniform(seeds[15], (1,), jnp.float32, 0.5, 1.5), 0.5, 1.5)
    return dict(tokens=tokens, segments=segments, gate_weight=gate_weight, value_weight=value_weight, coupling_weight=coupling_weight, step_weight=step_weight, value_conv=value_conv, coupling_conv=coupling_conv, value_shift=value_shift, coupling_shift=coupling_shift, step_bias=step_bias, decay_log=decay_log, skip_gain=skip_gain, norm_gain=norm_gain, out_weight=out_weight, rezero=rezero)


epsilon = 1e-05
highest = lax.Precision.HIGHEST

def stretch_update(state, previous, values, couple_in, couple_out, steps, decays, stretch_ids, per_group):
    length = values.shape[0]
    cumulative = jnp.cumsum(decays, axis=0)
    position = lax.broadcasted_iota(jnp.int32, (length, length), 0)
    source = lax.broadcasted_iota(jnp.int32, (length, length), 1)
    visible = jnp.logical_and(stretch_ids[:, None] == stretch_ids[None, :], position >= source)[:, :, None]
    spread = cumulative[:, None, :] - cumulative[None, :, :]
    damping = jnp.where(visible, jnp.exp(jnp.where(visible, spread, 0.0)), 0.0)
    scores = jnp.einsum('tgn,sgn->tsg', couple_out, couple_in, precision=highest)
    scores = jnp.repeat(scores, per_group, axis=2)
    mixing = scores * damping * steps[None, :, :]
    result = jnp.einsum('tsh,shp->thp', mixing, values, precision=highest)
    kept = (stretch_ids == previous).astype(jnp.float32)
    growth = kept[:, None] * jnp.exp(cumulative)
    query_heads = jnp.repeat(couple_out, per_group, axis=1)
    result = result + growth[:, :, None] * jnp.einsum('thn,hpn->thp', query_heads, state, precision=highest)
    tail_weight = (stretch_ids == stretch_ids[-1]).astype(jnp.float32)[:, None] * jnp.exp(cumulative[-1][None, :] - cumulative) * steps
    key_heads = jnp.repeat(couple_in, per_group, axis=1)
    renewed = growth[-1][:, None, None] * state + jnp.einsum('sh,shp,shn->hpn', tail_weight, values, key_heads, precision=highest)
    return (renewed, result, growth)

def causal_mix(padded, padded_ids, weight, shift_term):
    reach = weight.shape[0] - 1
    length = padded.shape[-2] - reach
    own_ids = padded_ids[..., reach:]
    running = jnp.zeros(padded[..., reach:, :].shape, jnp.float32) + shift_term.astype(jnp.float32)
    for offset in range(reach + 1):
        window = padded[..., offset:offset + length, :].astype(jnp.float32)
        matching = (padded_ids[..., offset:offset + length] == own_ids).astype(jnp.float32)
        running = running + weight[offset].astype(jnp.float32) * window * matching[..., None]
    return jax.nn.silu(running).astype(jnp.bfloat16)

def reference(tokens, segments, gate_weight, value_weight, coupling_weight, step_weight, value_conv, coupling_conv, value_shift, coupling_shift, step_bias, decay_log, skip_gain, norm_gain, out_weight, rezero):

    def one_stream(operands):
        stream_tokens, segment_ids = operands
        gate_proj = jnp.dot(stream_tokens, gate_weight, preferred_element_type=jnp.float32).astype(jnp.bfloat16)
        value_proj = jnp.dot(stream_tokens, value_weight, preferred_element_type=jnp.float32).astype(jnp.bfloat16)
        coupling_proj = jnp.dot(stream_tokens, coupling_weight, preferred_element_type=jnp.float32).astype(jnp.bfloat16)
        step_proj = jnp.dot(stream_tokens, step_weight, preferred_element_type=jnp.float32).astype(jnp.bfloat16)
        reach = value_conv.shape[0] - 1
        padded_ids = jnp.concatenate([jnp.full((reach,), -1, jnp.int32), segment_ids.astype(jnp.int32)])
        value_pad = jnp.concatenate([jnp.zeros((reach, value_proj.shape[1]), jnp.bfloat16), value_proj])
        coupling_pad = jnp.concatenate([jnp.zeros((reach, coupling_proj.shape[1]), jnp.bfloat16), coupling_proj])
        value_mixed = causal_mix(value_pad, padded_ids, value_conv, value_shift)
        coupling_mixed = causal_mix(coupling_pad, padded_ids, coupling_conv, coupling_shift)
        step_sizes = jax.nn.softplus(step_proj.astype(jnp.float32) + step_bias)
        decays = step_sizes * -jnp.exp(decay_log)
        values = value_mixed.astype(jnp.float32).reshape(LEN, H, P_SIZE)
        coupled = coupling_mixed.astype(jnp.float32).reshape(LEN, G, 2, N)
        couple_in = coupled[:, :, 0]
        couple_out = coupled[:, :, 1]
        stretches = LEN // CH

        def advance(carried, inputs):
            state, previous = carried
            stretch_values, stretch_in, stretch_out, stretch_steps, stretch_decays, stretch_ids = inputs
            renewed, result, growth = stretch_update(state, previous, stretch_values, stretch_in, stretch_out, stretch_steps, stretch_decays, stretch_ids, H // G)
            return ((renewed, stretch_ids[-1]), result)
        inputs = (values.reshape(stretches, CH, H, P_SIZE), couple_in.reshape(stretches, CH, G, N), couple_out.reshape(stretches, CH, G, N), step_sizes.reshape(stretches, CH, H), decays.reshape(stretches, CH, H), segment_ids.astype(jnp.int32).reshape(stretches, CH))
        initial = (jnp.zeros((H, P_SIZE, N), jnp.float32), jnp.array(-1, jnp.int32))
        finals, results = lax.scan(advance, initial, inputs)
        scanned = results.reshape(LEN, H, P_SIZE) + skip_gain[None, :, None] * values
        gated = scanned * jax.nn.silu(gate_proj.astype(jnp.float32)).reshape(LEN, H, P_SIZE)
        grouped = gated.reshape(LEN, G, H // G * P_SIZE)
        scale = lax.rsqrt(lax.optimization_barrier(jnp.mean(grouped * grouped, axis=-1, keepdims=True)) + epsilon)
        normed = ((grouped * scale).reshape(LEN, H * P_SIZE) * norm_gain).astype(jnp.bfloat16)
        branch = jnp.dot(normed, out_weight, preferred_element_type=jnp.float32)
        return (stream_tokens.astype(jnp.float32) + rezero[0] * branch).astype(jnp.bfloat16)
    return lax.map(one_stream, (tokens, segments))
```

```python
import jax
import jax.numpy as jnp
from jax import lax
from jax.experimental import pallas as pl
from jax.experimental.pallas import tpu as pltpu
from jax.sharding import PartitionSpec as P

P_SIZE = 64
N = 128
CH = 128
TAIL = 8
STATE_ROWS = N + 16
OUT_STEPS = 4

epsilon = 1e-05
highest = lax.Precision.HIGHEST
f32 = jnp.float32
bf16 = jnp.bfloat16
VMEM_LIMIT = 52 * 1024 * 1024


def dot(a, b):
    return jnp.dot(a, b, preferred_element_type=f32)


def turned(rows):
    fill = jnp.zeros((N - rows.shape[0], rows.shape[1]), f32)
    return jnp.concatenate([rows, fill], axis=0).T


def per_head(columns, first, heads):
    lane = lax.broadcasted_iota(jnp.int32, (columns.shape[0], 2 * P_SIZE), 1)
    low = lane < P_SIZE
    blocks = [
        jnp.where(low, columns[:, c : c + 1], columns[:, c + 1 : c + 2])
        for c in range(first, first + heads, 2)
    ]
    return jnp.concatenate(blocks, axis=1)


def spread_heads(columns, heads_per_step, steps):
    return jnp.concatenate(
        [per_head(columns, 8 * j, heads_per_step) for j in range(steps)], axis=1
    )


def mix_kernel(
    first_ref,
    second_ref,
    tails_ref,
    rows_ref,
    value_ref,
    coupling_ref,
    step_ref,
    value_conv_ref,
    coupling_conv_ref,
    value_shift_ref,
    coupling_shift_ref,
    head_ref,
    values_ref,
    coupled_ref,
    sums_ref,
    state_ref,
    rows_scr,
    step_scr,
    mask_scr,
    pad_scr,
):
    j = pl.program_id(0)
    steps = pl.num_programs(0)
    wide, narrow = value_ref.shape[1], coupling_ref.shape[1]
    heads = step_ref.shape[0]
    reach = value_conv_ref.shape[0] - 1

    @pl.when(j == 0)
    def _():
        rows_scr[0:CH] = first_ref[...]
        rows_scr[CH : 2 * CH] = second_ref[...]
        rows_scr[2 * CH : 2 * CH + 2 * TAIL] = tails_ref[...]
        step_scr[...] = lax.dot_general(
            step_ref[...],
            rows_scr[0 : 2 * CH],
            (((1,), (1,)), ((), ())),
            preferred_element_type=f32,
        )
        for s in range(2):
            mask_scr[s] = turned(rows_ref[s])

    def convolved(projected, taps_ref, shift_ref, out_ref, offset, width):
        projected = projected.astype(bf16).astype(f32)
        for s in range(2):
            pad_scr[0:TAIL, 0:width] = projected[2 * CH + TAIL * s : 2 * CH + TAIL * (s + 1)]
            pad_scr[TAIL : TAIL + CH, 0:width] = projected[CH * s : CH * (s + 1)]
            running = shift_ref[...] + taps_ref[reach : reach + 1].astype(f32) * projected[
                CH * s : CH * (s + 1)
            ]
            for k in range(reach):
                window = pad_scr[TAIL - reach + k : TAIL - reach + k + CH, 0:width]
                running = running + taps_ref[k : k + 1].astype(f32) * window * mask_scr[
                    s, :, k : k + 1
                ]
            out_ref[s, :, pl.ds(pl.multiple_of(offset, width), width)] = jax.nn.silu(
                running
            ).astype(bf16)

    rows = rows_scr[...]
    convolved(
        dot(rows, value_ref[...]), value_conv_ref, value_shift_ref, values_ref, j * wide, wide
    )
    convolved(
        dot(rows, coupling_ref[...]),
        coupling_conv_ref,
        coupling_shift_ref,
        coupled_ref,
        j * narrow,
        narrow,
    )

    @pl.when(j == steps - 1)
    def _():
        count = sums_ref.shape[1]
        per_step = heads // count
        groups = coupled_ref.shape[2] // (2 * N)
        share = values_ref.shape[2] // groups
        source = lax.broadcasted_iota(jnp.int32, (CH, CH), 0)
        position = lax.broadcasted_iota(jnp.int32, (CH, CH), 1)
        upto = (source <= position).astype(f32)
        for s in range(2):
            step_rows = step_scr[:, s * CH : (s + 1) * CH].astype(bf16).astype(f32)
            sizes = jax.nn.softplus(step_rows + head_ref[0])
            decays = -sizes * jnp.exp(head_ref[1])
            cumulative = jnp.dot(decays, upto, precision=highest, preferred_element_type=f32)
            last = cumulative[:, CH - 1 : CH]
            kept, ending = rows_ref[s, 4:5], rows_ref[s, 5:6]
            tail_weight = ending * jnp.exp(last - cumulative) * sizes
            growth = kept * jnp.exp(cumulative)
            gap = jnp.zeros((8 - per_step, CH), f32)
            spaced_tail, spaced_growth = [], []
            for jj in range(count):
                own = slice(jj * per_step, (jj + 1) * per_step)
                sums_ref[s, jj, 0:per_step] = cumulative[own]
                sums_ref[s, jj, per_step : 2 * per_step] = sizes[own]
                if 2 * per_step < 8:
                    sums_ref[s, jj, 2 * per_step : 8] = jnp.zeros((8 - 2 * per_step, CH), f32)
                spaced_tail += [tail_weight[own], gap]
                spaced_growth += [growth[own], gap]
            weights = spread_heads(
                turned(jnp.concatenate(spaced_tail, axis=0)), per_step, count
            )
            leading = spread_heads(
                turned(jnp.concatenate(spaced_growth, axis=0))[CH - 8 : CH], per_step, count
            )[7:8]
            weighted = (weights * values_ref[s].astype(f32)).astype(bf16)
            for g in range(groups):
                keys = coupled_ref[s, :, g * 2 * N : g * 2 * N + N]
                state_ref[s, 0:N, g * share : (g + 1) * share] = lax.dot_general(
                    keys,
                    weighted[:, g * share : (g + 1) * share],
                    (((0,), (0,)), ((), ())),
                    preferred_element_type=f32,
                ).astype(bf16)
            coarse = leading.astype(bf16).astype(f32)
            line = lax.broadcasted_iota(jnp.int32, (16, leading.shape[1]), 0)
            state_ref[s, N:STATE_ROWS] = jnp.where(
                line == 0, coarse, jnp.where(line == 1, leading - coarse, 0.0)
            ).astype(bf16)


def scan_kernel(
    first_ref,
    second_ref,
    rows_ref,
    gate_ref,
    values_ref,
    coupled_ref,
    sums_ref,
    skip_ref,
    gates_ref,
    local_ref,
    rows_scr,
    score_scr,
    hidden_scr,
):
    j = pl.program_id(0)
    groups = coupled_ref.shape[2] // (2 * N)
    per_step = values_ref.shape[2] // P_SIZE

    @pl.when(j == 0)
    def _():
        rows_scr[0:CH] = first_ref[...]
        rows_scr[CH : 2 * CH] = second_ref[...]
        position = lax.broadcasted_iota(jnp.int32, (CH, CH), 0)
        source = lax.broadcasted_iota(jnp.int32, (CH, CH), 1)
        for s in range(2):
            ids = turned(rows_ref[s])[:, 3:4]
            visible = jnp.logical_and(ids == rows_ref[s, 3:4], position >= source)
            hidden_scr[s] = jnp.where(visible, 0.0, -1e30)
            for g in range(groups):
                keys = coupled_ref[s, :, g * 2 * N : g * 2 * N + N]
                queries = coupled_ref[s, :, g * 2 * N + N : (g + 1) * 2 * N]
                score_scr[s, g] = lax.dot_general(
                    queries, keys, (((1,), (1,)), ((), ())), preferred_element_type=f32
                )

    projected = dot(rows_scr[...], gate_ref[...]).astype(bf16)
    lane = lax.broadcasted_iota(jnp.int32, (CH, 2 * P_SIZE), 1)
    group = j // 2
    for s in range(2):
        gates_ref[s] = projected[s * CH : (s + 1) * CH]
        columns = turned(sums_ref[s, 0])
        scores = score_scr[s, group]
        hidden = hidden_scr[s]
        for pair in range(per_step // 2):
            mixing = []
            for h in (2 * pair, 2 * pair + 1):
                damping = jnp.exp(columns[:, h : h + 1] - sums_ref[s, 0, h : h + 1] + hidden)
                sizes = sums_ref[s, 0, per_step + h : per_step + h + 1]
                mixing.append((scores * damping * sizes).astype(bf16))
            own = slice(pair * 2 * P_SIZE, (pair + 1) * 2 * P_SIZE)
            both = values_ref[s, :, own]
            mixed = dot(jnp.concatenate(mixing, axis=0), both)
            local_ref[s, :, own] = (
                jnp.where(lane < P_SIZE, mixed[0:CH], mixed[CH : 2 * CH])
                + skip_ref[:, own] * both.astype(f32)
            )


def out_kernel(
    local_ref,
    gates_ref,
    coupled_ref,
    sums_ref,
    rows_ref,
    entry_first_ref,
    entry_second_ref,
    gain_ref,
    out_ref,
    first_ref,
    second_ref,
    normed_scr,
):
    groups = coupled_ref.shape[2] // (2 * N)
    share = local_ref.shape[2] // groups
    count = sums_ref.shape[1]
    per_step = local_ref.shape[2] // P_SIZE // count

    @pl.when(pl.program_id(0) == 0)
    def _():
        for s, entry_ref in enumerate((entry_first_ref, entry_second_ref)):
            sums = jnp.concatenate([sums_ref[s, jj] for jj in range(count)], axis=0)
            line = lax.broadcasted_iota(jnp.int32, sums.shape, 0) % 8
            growth = rows_ref[s, 4:5] * jnp.exp(jnp.where(line < per_step, sums, 0.0))
            spread = spread_heads(turned(growth), per_step, count)
            for g in range(groups):
                own = slice(g * share, (g + 1) * share)
                queries = coupled_ref[s, :, g * 2 * N + N : (g + 1) * 2 * N]
                carried = dot(queries, entry_ref[:, own])
                scanned = local_ref[s, :, own] + spread[:, own] * carried
                gated = scanned * jax.nn.silu(gates_ref[s, :, own].astype(f32))
                scale = lax.rsqrt(jnp.mean(gated * gated, axis=-1, keepdims=True) + epsilon)
                normed_scr[s * CH : (s + 1) * CH, own] = (
                    gated * scale * gain_ref[:, own]
                ).astype(bf16)

    branch = dot(normed_scr[...], out_ref[...]).astype(bf16)
    first_ref[...] = branch[0:CH]
    second_ref[...] = branch[CH : 2 * CH]


def whole(a):
    return pl.BlockSpec(a.shape, lambda j: (0,) * a.ndim)


def columns_of(a, steps):
    lead = a.shape[:-1]
    return pl.BlockSpec((*lead, a.shape[-1] // steps), lambda j: (0,) * len(lead) + (j,))


def params():
    return pltpu.CompilerParams(
        dimension_semantics=("arbitrary",), vmem_limit_bytes=VMEM_LIMIT
    )


def cost(rows, *weights):
    flops = sum(2 * rows * w.shape[0] * w.shape[1] for w in weights)
    return pl.CostEstimate(
        flops=flops, bytes_accessed=sum(2 * w.size for w in weights), transcendentals=0
    )


def mix(first, second, tails, rows, weights, convs, head):
    value_weight, coupling_weight, step_rows = weights
    value_conv, coupling_conv, value_shift, coupling_shift = convs
    width, narrow, depth = value_weight.shape[1], coupling_weight.shape[1], first.shape[1]
    steps = narrow // N
    shapes = [
        jax.ShapeDtypeStruct((2, CH, width), bf16),
        jax.ShapeDtypeStruct((2, CH, narrow), bf16),
        jax.ShapeDtypeStruct((2, steps, 8, CH), f32),
        jax.ShapeDtypeStruct((2, STATE_ROWS, width), bf16),
    ]
    return pl.pallas_call(
        mix_kernel,
        grid=(steps,),
        in_specs=[
            whole(first),
            whole(second),
            whole(tails),
            whole(rows),
            columns_of(value_weight, steps),
            columns_of(coupling_weight, steps),
            whole(step_rows),
            columns_of(value_conv, steps),
            columns_of(coupling_conv, steps),
            columns_of(value_shift, steps),
            columns_of(coupling_shift, steps),
            whole(head),
        ],
        out_specs=[whole(s) for s in shapes],
        out_shape=shapes,
        scratch_shapes=[
            pltpu.VMEM((2 * CH + 2 * TAIL, depth), bf16),
            pltpu.VMEM((step_rows.shape[0], 2 * CH), f32),
            pltpu.VMEM((2, CH, CH), f32),
            pltpu.VMEM((CH + TAIL, width // steps), f32),
        ],
        compiler_params=params(),
        cost_estimate=cost(2 * CH, value_weight, coupling_weight),
        name="mix",
    )(
        first,
        second,
        tails,
        rows,
        value_weight,
        coupling_weight,
        step_rows,
        value_conv,
        coupling_conv,
        value_shift,
        coupling_shift,
        head,
    )


def scan(first, second, rows, gate_weight, values, coupled, sums, skip):
    shapes = [
        jax.ShapeDtypeStruct(values.shape, bf16),
        jax.ShapeDtypeStruct(values.shape, f32),
    ]
    steps = coupled.shape[2] // N
    return pl.pallas_call(
        scan_kernel,
        grid=(steps,),
        in_specs=[
            whole(first),
            whole(second),
            whole(rows),
            columns_of(gate_weight, steps),
            columns_of(values, steps),
            whole(coupled),
            pl.BlockSpec((2, 1, 8, CH), lambda j: (0, j, 0, 0)),
            columns_of(skip, steps),
        ],
        out_specs=[columns_of(s, steps) for s in shapes],
        out_shape=shapes,
        scratch_shapes=[
            pltpu.VMEM((2 * CH, first.shape[1]), bf16),
            pltpu.VMEM((2, steps // 2, CH, CH), f32),
            pltpu.VMEM((2, CH, CH), f32),
        ],
        compiler_params=params(),
        cost_estimate=cost(2 * CH, gate_weight),
        name="scan",
    )(first, second, rows, gate_weight, values, coupled, sums, skip)


def project_out(local, gates, coupled, sums, rows, entry_first, entry_second, gain, out_weight):
    depth = out_weight.shape[1]
    shapes = [jax.ShapeDtypeStruct((CH, depth), bf16)] * 2
    return pl.pallas_call(
        out_kernel,
        grid=(OUT_STEPS,),
        in_specs=[
            whole(local),
            whole(gates),
            whole(coupled),
            whole(sums),
            whole(rows),
            whole(entry_first),
            whole(entry_second),
            whole(gain),
            columns_of(out_weight, OUT_STEPS),
        ],
        out_specs=[columns_of(s, OUT_STEPS) for s in shapes],
        out_shape=shapes,
        scratch_shapes=[pltpu.VMEM((2 * CH, out_weight.shape[0]), bf16)],
        compiler_params=params(),
        cost_estimate=cost(2 * CH, out_weight),
        name="project_out",
    )(local, gates, coupled, sums, rows, entry_first, entry_second, gain, out_weight)


def along(block, axis, distance):
    devices = range(lax.axis_size(axis))
    return lax.ppermute(
        block, axis, [(i, i + distance) for i in devices if i + distance in devices]
    )


def partner(block, axis):
    return lax.ppermute(block, axis, [(i, i ^ 1) for i in range(lax.axis_size(axis))])


def rows_over(block, distance):
    size = lax.axis_size("fsdp")
    route = [(i, (i + 2 * distance) % size) for i in range(size)]
    return lax.ppermute(block, "fsdp", route)


def unpacked(block):
    block = block.astype(f32)
    return block[:N], block[N : N + 1] + block[N + 1 : N + 2]


def packed(state, factor):
    coarse = factor.astype(bf16).astype(f32)
    rest = jnp.zeros((STATE_ROWS - N - 2, state.shape[1]), f32)
    return jnp.concatenate([state, coarse, factor - coarse, rest], axis=0).astype(bf16)


def entry_states(ends):
    spans = lax.axis_size("ctx")
    odd = lax.axis_index("ctx") % 2 == 1
    given, kept = jnp.where(odd, ends[1], ends[0]), jnp.where(odd, ends[0], ends[1])
    got = partner(given, "ctx")
    even_state, even_factor = unpacked(jnp.where(odd, got, kept))
    odd_state, odd_factor = unpacked(jnp.where(odd, kept, got))
    state, factor = odd_state + odd_factor * even_state, odd_factor * even_factor
    distance = 1
    while distance < spans // 4:
        earlier_state, earlier_factor = unpacked(along(packed(state, factor), "ctx", 2 * distance))
        state, factor = state + factor * earlier_state, factor * earlier_factor
        distance *= 2
    before = along(state.astype(bf16), "ctx", 2)
    between = (even_state + even_factor * before.astype(f32)).astype(bf16)
    other = partner(jnp.where(odd, before, between), "ctx")
    own = jnp.where(odd, between, before)
    return jnp.where(odd, own, other), jnp.where(odd, other, own)


def on_device(
    tokens,
    segments,
    gate_weight,
    value_weight,
    coupling_weight,
    step_weight,
    value_conv,
    coupling_conv,
    value_shift,
    coupling_shift,
    step_bias,
    decay_log,
    skip_gain,
    norm_gain,
    out_weight,
    rezero,
):
    place = lax.axis_index("fsdp")
    streams = lax.axis_size("fsdp")
    chips = streams // 2
    chip, core = place // 2, place % 2
    reach = value_conv.shape[0] - 1
    own = tokens[0]

    tail = own[CH - TAIL :]
    tails = jnp.stack([tail] + [rows_over(tail, -d) for d in range(1, chips)])
    arrived = [own] + [rows_over(own, -d) for d in range(1, chips)]
    opposite = [partner(a, "fsdp") for a in arrived]
    tails = jnp.stack([tails, partner(tails, "fsdp")], axis=1)

    which = ((chip + jnp.arange(chips)) % chips * 2)[:, None] + (core ^ jnp.arange(2))[None, :]
    chosen = which[:, :, None] == jnp.arange(streams)[None, None, :]
    ids = jnp.sum(jnp.where(chosen[..., None], segments[None, None], 0), axis=2)
    last_ids = jnp.pad(
        ids[:, :, None, CH - TAIL :].astype(bf16),
        ((0, 0), (0, 0), (0, 0), (0, own.shape[1] - TAIL)),
    )
    tails = along(jnp.concatenate([last_ids, tails[:, :, 1:]], axis=2), "ctx", 1)
    prior_ids = tails[:, :, 0, TAIL - reach : TAIL].astype(jnp.int32)
    padded_ids = jnp.concatenate([prior_ids, ids], axis=2)
    rows = jnp.stack(
        [(padded_ids[:, :, k : k + CH] == ids).astype(f32) for k in range(reach)]
        + [
            ids.astype(f32),
            (ids == prior_ids[:, :, reach - 1 :]).astype(f32),
            (ids == ids[:, :, CH - 1 :]).astype(f32),
        ]
        + [jnp.zeros(ids.shape, f32)] * (8 - reach - 3),
        axis=2,
    )

    heads = step_weight.shape[1]
    head = jnp.broadcast_to(jnp.stack([step_bias, decay_log])[:, :, None], (2, heads, CH))
    skip = jnp.repeat(skip_gain, P_SIZE)[None]
    weights = (value_weight, coupling_weight, step_weight.T)
    convs = (value_conv, coupling_conv, value_shift[None], coupling_shift[None])

    partials = []
    for d in range(chips):
        pair = (arrived[d], opposite[d])
        values, coupled, sums, ends = mix(
            *pair, tails[d].reshape(2 * TAIL, -1), rows[d], weights, convs, head
        )
        entries = entry_states(ends)
        gates, local = scan(*pair, rows[d], gate_weight, values, coupled, sums, skip)
        partials.append(
            project_out(
                local, gates, coupled, sums, rows[d], *entries, norm_gain[None], out_weight
            )
        )
    branch = 0.0
    for d, (mine, others) in enumerate(partials):
        total = mine.astype(f32) + partner(others, "fsdp").astype(f32)
        if d:
            total = rows_over(total.astype(bf16), d).astype(f32)
        branch = branch + total
    return (own.astype(f32) + rezero[0] * branch).astype(bf16)[None]


def solution(mesh):
    return jax.shard_map(
        on_device,
        mesh=mesh,
        in_specs=(
            P("fsdp", "ctx", None),
            P(None, "ctx"),
            P(None, "fsdp"),
            P(None, "fsdp"),
            P(None, "fsdp"),
            P(None, "fsdp"),
            P(None, "fsdp"),
            P(None, "fsdp"),
            P("fsdp"),
            P("fsdp"),
            P("fsdp"),
            P("fsdp"),
            P("fsdp"),
            P("fsdp"),
            P("fsdp", None),
            P(),
        ),
        out_specs=P("fsdp", "ctx", None),
        check_vma=False,
    )
```

```python
import functools

import jax
import jax.numpy as jnp
from jax import lax
from jax.experimental import pallas as pl
from jax.experimental.pallas import tpu as pltpu
from jax.sharding import PartitionSpec as P

P_SIZE = 64
N = 128
CH = 128
HALF = CH // 2
TAIL = 8
TAILS = 16
WIDE = 256
PIECES = 4
STATE_ROWS = N + 16

epsilon = 1e-05
highest = lax.Precision.HIGHEST
f32 = jnp.float32
bf16 = jnp.bfloat16


def dot(a, b):
    return jnp.dot(a, b, preferred_element_type=f32)


def turned(rows):
    fill = jnp.zeros((N - rows.shape[0], rows.shape[1]), f32)
    return jnp.concatenate([rows, fill], axis=0).T


def per_head(columns, first, heads):
    lane = lax.broadcasted_iota(jnp.int32, (columns.shape[0], 2 * P_SIZE), 1)
    low = lane < P_SIZE
    blocks = [
        jnp.where(low, columns[:, c : c + 1], columns[:, c + 1 : c + 2])
        for c in range(first, first + heads, 2)
    ]
    return jnp.concatenate(blocks, axis=1)


def spread_heads(columns, heads_per_step, steps):
    return jnp.concatenate(
        [per_head(columns, 8 * j, heads_per_step) for j in range(steps)], axis=1
    )


def fill_rows(rows_scr, sources, core, flip):
    if flip is None:
        rows_scr[0:CH] = sources[0][...]
        rows_scr[CH : 2 * CH] = sources[1][...]
        return
    for ref, taken in zip(sources, (core == flip, core != flip)):

        @pl.when(taken)
        def _(ref=ref):
            rows_scr[0:CH] = ref[...]


def ids_row(flags_ref, segments_ref, at):
    ids = segments_ref[...].astype(f32)
    line = lax.broadcasted_iota(jnp.int32, ids.shape, 0)
    return jnp.sum(jnp.where(line == flags_ref[at], ids, 0.0), axis=0, keepdims=True)


def tail_kernel(flags_ref, own_ref, segments_ref, after_ref, tail_ref):
    del after_ref
    tail_ref[...] = own_ref[CH - TAILS : CH]
    line = lax.broadcasted_iota(jnp.int32, (TAILS, CH), 0)
    tail_ref[:, 0:CH] = jnp.where(
        line == 0,
        ids_row(flags_ref, segments_ref, 3),
        own_ref[CH - TAILS : CH, 0:CH].astype(f32),
    ).astype(bf16)


def facts(rows_ref, s, ids, prior, reach):
    lane = lax.broadcasted_iota(jnp.int32, (8, CH), 1)
    line = lax.broadcasted_iota(jnp.int32, (8, CH), 0)
    ids, prior = (jnp.broadcast_to(a, (8, CH)) for a in (ids, prior))
    found = jnp.zeros((8, CH), f32)
    for k in range(reach):
        back = reach - k
        earlier = jnp.where(lane < back, pltpu.roll(prior, back, 1), pltpu.roll(ids, back, 1))
        found = jnp.where(line == k, jnp.where(earlier == ids, 1.0, 0.0), found)
    found = jnp.where(line == 3, ids, found)
    found = jnp.where(line == 4, jnp.where(ids == prior[:, CH - 1 : CH], 1.0, 0.0), found)
    found = jnp.where(line == 5, jnp.where(ids == ids[:, CH - 1 : CH], 1.0, 0.0), found)
    rows_ref[s] = found


def mix_kernel(slots, streams, flip, flags_ref, *refs):
    sources, refs = refs[:2], refs[2:]
    tail_refs, refs = refs[:2], refs[-(12 + slots) :]
    segments_ref, value_ref, coupling_ref, step_ref, taps_ref, head_ref = refs[:6]
    refs = refs[6:]
    values_ref, coupled_ref, sums_ref, rows_ref = refs[:4]
    state_refs, (rows_scr, pad_scr) = refs[4 : 4 + slots], refs[4 + slots :]
    odd = flags_ref[0] == 1
    heads = step_ref.shape[0]
    reach = 3
    count = sums_ref.shape[1]
    per_step = heads // count
    width = values_ref.shape[2]
    groups = coupled_ref.shape[2] // (2 * N)
    share = width // groups
    held = slots * CH

    work = []
    for g in range(groups):
        work.append((coupling_ref, coupled_ref, width, g))
        for piece in range(share // WIDE):
            work.append((value_ref, values_ref, 0, g * (share // WIDE) + piece))
    fill_rows(rows_scr, sources, flags_ref[1], flip)
    later = flags_ref[2] > 0
    tails = [ref[...].astype(f32) for ref in tail_refs]
    if slots == 1:
        tails = [jnp.where(flags_ref[1] == flip, tails[0], tails[1])]
    for s, tail in enumerate(tails):
        tail = jnp.where(later, tail, 0.0)
        rows_scr[held + TAILS * s : held + TAILS * (s + 1)] = tail.astype(bf16)
        facts(rows_ref, s, ids_row(flags_ref, segments_ref, streams[s]), tail[0:1, 0:CH], reach)
    masks = [turned(rows_ref[s]) for s in range(slots)]
    rows = rows_scr[...]
    step_rows = lax.dot_general(
        step_ref[...], rows_scr[0:held], (((1,), (1,)), ((), ())), preferred_element_type=f32
    )

    def convolved(projected, out_ref, base, at, slot):
        projected = projected.astype(bf16).astype(f32)
        taps = taps_ref[:, base + at * WIDE : base + (at + 1) * WIDE]
        for s in range(slots):
            body = projected[CH * s : CH * (s + 1)]
            start = held + TAILS * (s + 1) - TAIL
            pad_scr[slot, s, 0:TAIL] = projected[start : start + TAIL]
            pad_scr[slot, s, TAIL : TAIL + CH] = body
            running = taps[reach + 1 : reach + 2] + taps[reach : reach + 1] * body
            for k in range(reach):
                window = pad_scr[slot, s, TAIL - reach + k : TAIL - reach + k + CH]
                running = running + taps[k : k + 1] * window * masks[s][:, k : k + 1]
            out_ref[s, :, at * WIDE : (at + 1) * WIDE] = jax.nn.silu(running).astype(bf16)

    source = lax.broadcasted_iota(jnp.int32, (CH, CH), 0)
    position = lax.broadcasted_iota(jnp.int32, (CH, CH), 1)
    upto = (source <= position).astype(f32)

    def put_states(parts, lines, columns):
        if slots == 2:
            parts = [jnp.where(odd, parts[1], parts[0]), jnp.where(odd, parts[0], parts[1])]
        for ref, part in zip(state_refs, parts):
            ref[lines, columns] = part.astype(bf16)

    def weighed(s):
        sizes = jax.nn.softplus(
            step_rows[:, s * CH : (s + 1) * CH].astype(bf16).astype(f32) + head_ref[0]
        )
        decays = -sizes * jnp.exp(head_ref[1])
        cumulative = jnp.dot(decays, upto, precision=highest, preferred_element_type=f32)
        last = cumulative[:, CH - 1 : CH]
        kept, ending = rows_ref[s, 4:5], rows_ref[s, 5:6]
        tail_weight = ending * jnp.exp(last - cumulative) * sizes
        growth = kept * jnp.exp(cumulative)
        gap = jnp.zeros((8 - per_step, CH), f32)
        spaced_tail, spaced_growth = [], []
        for jj in range(count):
            own = slice(jj * per_step, (jj + 1) * per_step)
            sums_ref[s, jj, 0:per_step] = cumulative[own]
            sums_ref[s, jj, per_step : 2 * per_step] = sizes[own]
            spaced_tail += [tail_weight[own], gap]
            spaced_growth += [growth[own], gap]
        leading = spread_heads(
            turned(jnp.concatenate(spaced_growth, axis=0))[CH - 8 : CH], per_step, count
        )[7:8]
        coarse = leading.astype(bf16).astype(f32)
        line = lax.broadcasted_iota(jnp.int32, (STATE_ROWS - N, width), 0)
        factor = jnp.where(line == 0, coarse, jnp.where(line == 1, leading - coarse, 0.0))
        return turned(jnp.concatenate(spaced_tail, axis=0)), factor

    def ended(g):
        own = slice(g * share, (g + 1) * share)
        parts = []
        for s in range(slots):
            part = spread_heads(
                weights[s][0][:, g * 8 * count // groups : (g + 1) * 8 * count // groups],
                per_step,
                count // groups,
            )
            weighted = (part * values_ref[s, :, own].astype(f32)).astype(bf16)
            keys = coupled_ref[s, :, g * 2 * N : g * 2 * N + N]
            parts.append(
                lax.dot_general(
                    keys, weighted, (((0,), (0,)), ((), ())), preferred_element_type=f32
                )
            )
        put_states(parts, slice(0, N), own)

    weights = [weighed(s) for s in range(slots)]
    put_states([w[1] for w in weights], slice(N, STATE_ROWS), slice(0, width))
    per_group = len(work) // groups
    waiting = None
    for i in range(len(work) + 1):
        following = None
        if i < len(work):
            weight_ref, out_ref, base, at = work[i]
            following = (
                dot(rows, weight_ref[:, at * WIDE : (at + 1) * WIDE]),
                out_ref,
                base,
                at,
                i % 2,
            )
        if waiting is not None:
            convolved(*waiting)
            if i % per_group == 0:
                ended(i // per_group - 1)
        waiting = following


def scan_kernel(slots, flip, flags_ref, *refs):
    sources, refs = refs[:2], refs[2:]
    (
        rows_ref,
        gate_ref,
        values_ref,
        coupled_ref,
        sums_ref,
        skip_ref,
        gates_ref,
        local_ref,
        rows_scr,
    ) = refs
    count = sums_ref.shape[1]
    groups = coupled_ref.shape[2] // (2 * N)
    per_step = WIDE // P_SIZE
    fill_rows(rows_scr, sources, flags_ref[1], flip)
    rows = rows_scr[...]
    position = lax.broadcasted_iota(jnp.int32, (CH, CH), 0)
    source = lax.broadcasted_iota(jnp.int32, (CH, CH), 1)
    lane = lax.broadcasted_iota(jnp.int32, (CH, 2 * P_SIZE), 1)
    hidden = []
    for s in range(slots):
        ids = turned(rows_ref[s])[:, 3:4]
        visible = jnp.logical_and(ids == rows_ref[s, 3:4], position >= source)
        hidden.append(jnp.where(visible, 0.0, -1e30))
    scores = None
    for j in range(count):
        if j % (count // groups) == 0:
            g = j // (count // groups)
            scores = [
                lax.dot_general(
                    coupled_ref[s, :, g * 2 * N + N : (g + 1) * 2 * N],
                    coupled_ref[s, :, g * 2 * N : g * 2 * N + N],
                    (((1,), (1,)), ((), ())),
                    preferred_element_type=f32,
                )
                for s in range(slots)
            ]
        for s in range(slots):
            columns = turned(sums_ref[s, j])
            for pair in range(per_step // 2):
                mixing = []
                for h in (2 * pair, 2 * pair + 1):
                    damping = jnp.exp(
                        columns[:, h : h + 1] - sums_ref[s, j, h : h + 1] + hidden[s]
                    )
                    sizes = sums_ref[s, j, per_step + h : per_step + h + 1]
                    mixing.append((scores[s] * damping * sizes).astype(bf16))
                own = slice(j * WIDE + pair * 2 * P_SIZE, j * WIDE + (pair + 1) * 2 * P_SIZE)
                both = values_ref[s, :, own]
                mixed = dot(jnp.concatenate(mixing, axis=0), both)
                local_ref[s, :, own] = (
                    jnp.where(lane < P_SIZE, mixed[0:CH], mixed[CH : 2 * CH])
                    + per_head(skip_ref[...], j * per_step + 2 * pair, 2) * both.astype(f32)
                )
        own = slice(j * WIDE, (j + 1) * WIDE)
        projected = dot(rows, gate_ref[:, own]).astype(bf16)
        for s in range(slots):
            gates_ref[s, :, own] = projected[s * CH : (s + 1) * CH]


def unpacked(state, tail):
    tail = tail.astype(f32)
    return state.astype(f32), tail[0:1] + tail[1:2]


def paired(odd, mine_ref, got_ref):
    lines = (slice(0, N), slice(N, STATE_ROWS))
    mine, got = [[ref[line] for line in lines] for ref in (mine_ref, got_ref)]
    even = [jnp.where(odd, g.astype(f32), m.astype(f32)) for m, g in zip(mine, got)]
    later = [jnp.where(odd, m.astype(f32), g.astype(f32)) for m, g in zip(mine, got)]
    return unpacked(*even), unpacked(*later)


def put_packed(out_ref, state, factor):
    out_ref[0:N] = state.astype(bf16)
    if out_ref.shape[0] > N:
        coarse = factor.astype(bf16).astype(f32)
        line = lax.broadcasted_iota(jnp.int32, (STATE_ROWS - N, state.shape[1]), 0)
        out_ref[N:STATE_ROWS] = jnp.where(
            line == 0, coarse, jnp.where(line == 1, factor - coarse, 0.0)
        ).astype(bf16)


def join_kernel(flags_ref, mine_ref, got_ref, out_ref):
    even, later = paired(flags_ref[0] == 1, mine_ref, got_ref)
    put_packed(out_ref, later[0] + later[1] * even[0], later[1] * even[1])


def chain_kernel(distance, flags_ref, mine_ref, got_ref, out_ref):
    state, factor = unpacked(mine_ref[0:N], mine_ref[N:STATE_ROWS])
    earlier, leading = unpacked(got_ref[0:N], got_ref[N:STATE_ROWS])
    reached = jnp.where(flags_ref[2] >= distance, factor, 0.0)
    put_packed(out_ref, state + reached * earlier, reached * leading)


def entered(flags_ref, mine_ref, got_ref, before_ref):
    even, _ = paired(flags_ref[0] == 1, mine_ref, got_ref)
    before = jnp.where(flags_ref[2] >= 2, before_ref[...].astype(f32), 0.0)
    return before, even[0] + even[1] * before


def finish_kernel(flags_ref, mine_ref, got_ref, before_ref, own_ref, other_ref):
    odd = flags_ref[0] == 1
    before, between = entered(flags_ref, mine_ref, got_ref, before_ref)
    own_ref[...] = jnp.where(odd, between, before).astype(bf16)
    other_ref[...] = jnp.where(odd, before, between).astype(bf16)


def out_kernel(slots, blocks, flags_ref, *refs):
    entry_refs, refs = refs[: 4 - slots], refs[4 - slots :]
    (
        local_ref,
        gates_ref,
        coupled_ref,
        sums_ref,
        rows_ref,
        gain_ref,
        out_ref,
        first_ref,
        *second_refs,
        normed_scr,
    ) = refs
    wide = out_ref.shape[1] // blocks
    odd = flags_ref[0] == 1
    groups = coupled_ref.shape[2] // (2 * N)
    share = local_ref.shape[2] // groups
    count = sums_ref.shape[1]
    per_step = WIDE // P_SIZE
    if slots == 1:
        before, between = entered(flags_ref, *entry_refs)
        entries = [jnp.where(odd, between, before).astype(bf16)]
    else:
        own, other = [ref[...].astype(f32) for ref in entry_refs]
        entries = [jnp.where(odd, own, other).astype(bf16), jnp.where(odd, other, own).astype(bf16)]
    for s in range(slots):
        sums = jnp.concatenate([sums_ref[s, jj] for jj in range(count)], axis=0)
        line = lax.broadcasted_iota(jnp.int32, sums.shape, 0) % 8
        growth = rows_ref[s, 4:5] * jnp.exp(jnp.where(line < per_step, sums, 0.0))
        spread = spread_heads(turned(growth), per_step, count)
        for g in range(groups):
            own = slice(g * share, (g + 1) * share)
            queries = coupled_ref[s, :, g * 2 * N + N : (g + 1) * 2 * N]
            carried = dot(queries, entries[s][:, own])
            scanned = local_ref[s, :, own] + spread[:, own] * carried
            gated = scanned * jax.nn.silu(gates_ref[s, :, own].astype(f32))
            scale = lax.rsqrt(jnp.mean(gated * gated, axis=-1, keepdims=True) + epsilon)
            normed_scr[s * CH : (s + 1) * CH, own] = (gated * scale * gain_ref[:, own]).astype(
                bf16
            )

    normed = normed_scr[...]
    low = flags_ref[1] == 0
    for j in range(blocks):
        own = slice(j * wide, (j + 1) * wide)
        branch = dot(normed, out_ref[:, own])
        if slots == 2:
            first_ref[:, own] = branch[0:CH].astype(bf16)
            second_refs[0][:, own] = branch[CH : 2 * CH].astype(bf16)
        else:
            upper, lower = branch[0:HALF], branch[HALF:CH]
            first_ref[:, own] = jnp.where(low, upper, lower).astype(bf16)
            per_piece = blocks // len(second_refs)
            at = j % per_piece
            second_refs[j // per_piece][:, at * wide : (at + 1) * wide] = jnp.where(
                low, lower, upper
            ).astype(bf16)


def summed(refs):
    return sum(ref[...].astype(f32) for ref in refs)


def add_kernel(flags_ref, mine_ref, *refs):
    del flags_ref
    *other_refs, out_ref = refs
    wide = out_ref.shape[1] // len(other_refs)
    for j, ref in enumerate(other_refs):
        own = slice(j * wide, (j + 1) * wide)
        out_ref[:, own] = (mine_ref[:, own].astype(f32) + ref[...].astype(f32)).astype(bf16)


def give_kernel(flags_ref, *refs):
    *back, out_ref = refs
    chips = len(back) // 2
    out_ref[...] = jnp.where(
        flags_ref[1] == 0, summed(back[chips:]), summed(back[:chips])
    ).astype(bf16)


def close_kernel(flags_ref, rezero_ref, own_ref, mine_ref, others_ref, theirs_ref, *refs):
    *back, out_ref = refs
    chips = len(back) // 2
    core = flags_ref[1]
    ours = jnp.where(core == 0, summed(back[:chips]), summed(back[chips:]))
    for at, far in ((core, ours), (1 - core, theirs_ref[...].astype(f32))):
        lines = pl.ds(pl.multiple_of(at * HALF, HALF), HALF)
        branch = mine_ref[lines].astype(f32) + others_ref[lines].astype(f32) + far
        out_ref[lines] = (own_ref[lines].astype(f32) + rezero_ref[0] * branch).astype(bf16)


IN_VMEM = pl.BlockSpec(memory_space=pltpu.VMEM)
IN_SMEM = pl.BlockSpec(memory_space=pltpu.SMEM)
FLOPS_PER_US = 1_150_000_000


class Sequence:
    def __init__(self, flags):
        self.flags, self.token = flags, None

    def run(self, kernel, name, shapes, scratch, *operands, mib=2, us=1, scalars=()):
        tokens = [] if self.token is None else [self.token]
        given = 1 + len(scalars) + len(operands)

        def ordered(*refs):
            outs = refs[given + len(tokens) :]
            mark_ref = outs[len(shapes)]
            mark_ref[...] = jnp.zeros_like(mark_ref)
            kernel(*refs[:given], *outs[: len(shapes)], *outs[len(shapes) + 1 :])

        *results, self.token = pl.pallas_call(
            ordered,
            in_specs=[IN_SMEM] * (1 + len(scalars)) + [IN_VMEM] * (len(operands) + len(tokens)),
            out_specs=[IN_VMEM] * (len(shapes) + 1),
            out_shape=[*shapes, shape(f32, 8, CH)],
            scratch_shapes=scratch,
            compiler_params=pltpu.CompilerParams(vmem_limit_bytes=mib << 20),
            cost_estimate=pl.CostEstimate(
                flops=int(us * FLOPS_PER_US), bytes_accessed=0, transcendentals=0
            ),
            name=name,
        )(self.flags, *scalars, *operands, *tokens)
        return results

    def held(self, block):
        def hold(block_ref, token_ref, out_ref):
            del block_ref, token_ref, out_ref

        return pl.pallas_call(
            hold,
            in_specs=[IN_VMEM] * 2,
            out_specs=IN_VMEM,
            out_shape=shape(block.dtype, *block.shape),
            input_output_aliases={0: 0},
            compiler_params=pltpu.CompilerParams(vmem_limit_bytes=1 << 20),
            name="hold",
        )(block, self.token)


def shape(dtype, *sizes):
    return jax.ShapeDtypeStruct(sizes, dtype)


def mix(run, slots, streams, flip, sources, tails, segments, weights, small):
    value_weight, coupling_weight = weights
    width, narrow, depth = value_weight.shape[1], coupling_weight.shape[1], tails[0].shape[1]
    shapes = [
        shape(bf16, slots, CH, width),
        shape(bf16, slots, CH, narrow),
        shape(f32, slots, narrow // N, 8, CH),
        shape(f32, slots, 8, CH),
    ] + [shape(bf16, STATE_ROWS, width)] * slots
    scratch = [
        pltpu.VMEM((slots * (CH + TAILS), depth), bf16),
        pltpu.VMEM((2, slots, CH + TAIL, WIDE), f32),
    ]
    kernel = functools.partial(mix_kernel, slots, streams, flip)
    operands = (*sources, *tails, segments, *weights, *small)
    return run(kernel, f"mix{slots}", shapes, scratch, *operands, mib=8, us=4 * slots)


def scan(run, slots, flip, sources, rows, gate_weight, values, coupled, sums, skip):
    shapes = [shape(bf16, *values.shape), shape(f32, *values.shape)]
    scratch = [pltpu.VMEM((slots * CH, gate_weight.shape[0]), bf16)]
    kernel = functools.partial(scan_kernel, slots, flip)
    operands = (*sources, rows, gate_weight, values, coupled, sums, skip)
    return run(kernel, f"scan{slots}", shapes, scratch, *operands, mib=6, us=2 * slots)


def project_out(run, slots, entries, local, gates, coupled, sums, rows, gain, out_weight):
    width, depth = out_weight.shape
    lines = CH if slots == 2 else HALF
    scratch = [pltpu.VMEM((slots * CH, width), bf16)]
    kernel = functools.partial(out_kernel, slots, 8)
    operands = (*entries, local, gates, coupled, sums, rows, gain, out_weight)
    pieces = 1 if slots == 2 else PIECES
    shapes = [shape(bf16, lines, depth)] + [shape(bf16, lines, depth // pieces)] * pieces
    return run(kernel, f"out{slots}", shapes, scratch, *operands, mib=6, us=0.1)


def along(block, distance):
    spans = lax.axis_size("ctx")
    return lax.ppermute(block, "ctx", [(i, (i + distance) % spans) for i in range(spans)])


def tail_from(block, chips_on, flip):
    places, spans = lax.axis_size("fsdp"), lax.axis_size("ctx")
    route = [
        (((f + 2 * chips_on) % places ^ flip) * spans + c, f * spans + (c + 1) % spans)
        for f in range(places)
        for c in range(spans)
    ]
    return lax.ppermute(block, ("fsdp", "ctx"), route)


def partner(block, axis):
    return lax.ppermute(block, axis, [(i, i ^ 1) for i in range(lax.axis_size(axis))])


def over(block, distance):
    size = lax.axis_size("fsdp")
    return lax.ppermute(block, "fsdp", [(i, (i + 2 * distance) % size) for i in range(size)])


def joined(run, mine, got):
    return run(join_kernel, "join", [shape(bf16, *mine.shape)], [], mine, got, us=0.1)[0]


def chained(run, block):
    spans, width = lax.axis_size("ctx"), block.shape[1]
    distance = 2
    while distance < spans // 2:
        last = 2 * distance >= spans // 2
        out = [shape(bf16, N if last else STATE_ROWS, width)]
        kernel = functools.partial(chain_kernel, distance)
        block = run(kernel, "chain", out, [], block, along(block, distance), us=0.1)[0]
        distance *= 2
    return block


def on_device(
    tokens,
    segments,
    gate_weight,
    value_weight,
    coupling_weight,
    step_weight,
    value_conv,
    coupling_conv,
    value_shift,
    coupling_shift,
    step_bias,
    decay_log,
    skip_gain,
    norm_gain,
    out_weight,
    rezero,
):
    place = lax.axis_index("fsdp")
    span = lax.axis_index("ctx")
    chips = lax.axis_size("fsdp") // 2
    chip, core = place // 2, place % 2
    reach = value_conv.shape[0] - 1
    own = tokens[0]
    phases = [(d, j) for d in range(1, chips) for j in range(2)]
    far_streams = [(chip + d) % chips * 2 + j for d, j in phases]
    flags = jnp.stack([span % 2, core, span, place, place ^ 1] + far_streams).astype(jnp.int32)

    sequence = Sequence(flags)
    run = sequence.run

    arrived = {d: over(own, -d) for d in range(1, chips)}
    opposite = partner(own, "fsdp")
    half_shape = shape(bf16, HALF, own.shape[1])
    tail_shape = shape(bf16, TAILS, own.shape[1])
    tail = run(tail_kernel, "tail", [tail_shape], [], own, segments, opposite, us=8)[0]

    heads = step_weight.shape[1]
    head = jnp.broadcast_to(jnp.stack([step_bias, decay_log])[:, :, None], (2, heads, CH))
    skip = skip_gain[None]
    taps = jnp.concatenate([value_conv, coupling_conv], axis=1).astype(f32)
    shifts = jnp.concatenate([value_shift, coupling_shift])[None]
    taps = jnp.concatenate([taps, shifts, jnp.zeros((4 - reach, taps.shape[1]), f32)], axis=0)
    small = (step_weight.T, taps, head)
    gain = norm_gain[None]

    weights = (value_weight, coupling_weight)
    near = [tail_from(tail, 0, flip) for flip in range(2)]
    far = {d: [tail_from(tail, d, flip) for flip in range(2)] for d in range(1, chips)}
    near_sources = (own, opposite)
    values, coupled, near_sums, near_rows, given, kept = mix(
        run, 2, (3, 4), None, near_sources, near + sum(far.values(), []), segments, weights, small
    )
    near_mixed = (values, coupled, near_sums)
    near_got = partner(given, "ctx")

    far_mixed = []
    for i, (d, j) in enumerate(phases):
        if j == 0:
            arrival = sequence.held(arrived[d])
            sources = (arrival, partner(arrival, "fsdp"))
        *mixed, state = mix(run, 1, (5 + i,), j, sources, far[d], segments, weights, small)
        far_mixed.append((sources, *mixed, state, partner(state, "ctx")))
        if i == 0:
            near_block = joined(run, kept, near_got)

    far_scans, blocks = [], []
    for (d, j), (sources, values, coupled, sums, rows, state, got) in zip(phases, far_mixed):
        blocks.append(joined(run, state, got))
        far_scans.append(
            scan(run, 1, j, sources, rows, gate_weight, values, coupled, sums, skip)
        )
        if len(blocks) == 1:
            near_before = along(chained(run, near_block), 2)
    near_gates, near_local = scan(
        run, 2, None, near_sources, near_rows, gate_weight, *near_mixed, skip
    )
    entry_shape = shape(bf16, N, kept.shape[1])
    befores = []
    for block in blocks:
        befores.append(along(chained(run, block), 2))
        if len(befores) == 1:
            entry, other_entry = run(
                finish_kernel, "finish", [entry_shape] * 2, [], kept, near_got, near_before, us=0.1
            )
    near_entries = (entry, partner(other_entry, "ctx"))

    back = {}
    for (d, j), before, (gates, local), (_, _, coupled, sums, rows, state, got) in zip(
        phases, befores, far_scans, far_mixed
    ):
        mine, *others = project_out(
            run, 1, (state, got, before), local, gates, coupled, sums, rows, gain, out_weight
        )
        others = [partner(piece, "fsdp") for piece in others]
        total = run(add_kernel, "add", [half_shape], [], mine, *others, us=0.1)[0]
        back[d, j] = over(total, d)

    mine, others = project_out(
        run,
        2,
        near_entries,
        near_local,
        near_gates,
        near_mixed[1],
        near_sums,
        near_rows,
        gain,
        out_weight,
    )
    others = partner(others, "fsdp")
    returned = [back[d, j] for j in range(2) for d in range(1, chips)]
    given = run(give_kernel, "give", [half_shape], [], *returned, us=0.1)[0]
    return run(
        close_kernel,
        "close",
        [shape(bf16, *own.shape)],
        [],
        own,
        mine,
        others,
        partner(given, "fsdp"),
        *returned,
        mib=4,
        scalars=(rezero,),
    )[0][None]


def solution(mesh):
    return jax.shard_map(
        on_device,
        mesh=mesh,
        in_specs=(
            P("fsdp", "ctx", None),
            P(None, "ctx"),
            P(None, "fsdp"),
            P(None, "fsdp"),
            P(None, "fsdp"),
            P(None, "fsdp"),
            P(None, "fsdp"),
            P(None, "fsdp"),
            P("fsdp"),
            P("fsdp"),
            P("fsdp"),
            P("fsdp"),
            P("fsdp"),
            P("fsdp"),
            P("fsdp", None),
            P(),
        ),
        out_specs=P("fsdp", "ctx", None),
        check_vma=False,
    )
```

```python
import functools

import jax
import jax.numpy as jnp
from jax import lax
from jax.experimental import pallas as pl
from jax.experimental.pallas import tpu as pltpu
from jax.sharding import PartitionSpec as P

P_SIZE = 64
N = 128
CH = 128
HALF = CH // 2
TAIL = 8
TAILS = 16
WIDE = 256
PIECES = 4
FACTOR_ROWS = 16

epsilon = 1e-05
highest = lax.Precision.HIGHEST
f32 = jnp.float32
bf16 = jnp.bfloat16


def dot(a, b):
    return jnp.dot(a, b, preferred_element_type=f32)


def turned(rows):
    fill = jnp.zeros((N - rows.shape[0], rows.shape[1]), f32)
    return jnp.concatenate([rows, fill], axis=0).T


def per_head(columns, first, heads):
    lane = lax.broadcasted_iota(jnp.int32, (columns.shape[0], 2 * P_SIZE), 1)
    low = lane < P_SIZE
    blocks = [
        jnp.where(low, columns[:, c : c + 1], columns[:, c + 1 : c + 2])
        for c in range(first, first + heads, 2)
    ]
    return jnp.concatenate(blocks, axis=1)


def spread_heads(columns, heads_per_step, steps):
    return jnp.concatenate(
        [per_head(columns, 8 * j, heads_per_step) for j in range(steps)], axis=1
    )


def fill_rows(rows_scr, sources, core, flip):
    if flip is None:
        rows_scr[0:CH] = sources[0][...]
        rows_scr[CH : 2 * CH] = sources[1][...]
        return
    for ref, taken in zip(sources, (core == flip, core != flip)):

        @pl.when(taken)
        def _(ref=ref):
            rows_scr[0:CH] = ref[...]


def ids_row(flags_ref, segments_ref, at):
    ids = segments_ref[...].astype(f32)
    line = lax.broadcasted_iota(jnp.int32, ids.shape, 0)
    return jnp.sum(jnp.where(line == flags_ref[at], ids, 0.0), axis=0, keepdims=True)


def tail_kernel(flags_ref, own_ref, opposite_ref, segments_ref, tail_ref):
    half = tail_ref.shape[1]
    own, opposite = (
        ref[CH - TAILS : CH].astype(f32)[TAILS - TAIL :] for ref in (own_ref, opposite_ref)
    )
    line = lax.broadcasted_iota(jnp.int32, own.shape, 0)
    both = jnp.where(line < TAIL // 2, pltpu.roll(own, TAIL // 2, 0), opposite)
    line = line[:, 0:CH]
    labelled = jnp.where(
        line == 0,
        ids_row(flags_ref, segments_ref, 3),
        jnp.where(line == TAIL // 2, ids_row(flags_ref, segments_ref, 4), both[:, 0:CH]),
    )
    both = jnp.concatenate([labelled, both[:, CH:]], axis=1)
    tail_ref[...] = jnp.concatenate([both[:, :half], both[:, half:]]).astype(bf16)


def facts(rows_ref, s, ids, prior, reach):
    lane = lax.broadcasted_iota(jnp.int32, (8, CH), 1)
    line = lax.broadcasted_iota(jnp.int32, (8, CH), 0)
    ids, prior = (jnp.broadcast_to(a, (8, CH)) for a in (ids, prior))
    found = jnp.zeros((8, CH), f32)
    for k in range(reach):
        back = reach - k
        earlier = jnp.where(lane < back, pltpu.roll(prior, back, 1), pltpu.roll(ids, back, 1))
        found = jnp.where(line == k, jnp.where(earlier == ids, 1.0, 0.0), found)
    found = jnp.where(line == 3, ids, found)
    found = jnp.where(line == 4, jnp.where(ids == prior[:, CH - 1 : CH], 1.0, 0.0), found)
    found = jnp.where(line == 5, jnp.where(ids == ids[:, CH - 1 : CH], 1.0, 0.0), found)
    rows_ref[s] = found


def mix_kernel(slots, streams, flip, carried, flags_ref, *refs):
    sources, refs = refs[:2], refs[2:]
    tail_ref, refs = refs[0], refs[-15 - carried :]
    segments_ref, value_ref, coupling_ref, step_ref, *taps_refs, head_ref = refs[:9]
    refs = refs[9:]
    values_ref, coupled_ref, sums_ref, rows_ref = refs[:4]
    state_refs, (rows_scr, pad_scr) = refs[4 : 4 + carried], refs[4 + carried :]
    lines = state_refs[0].shape[0] - FACTOR_ROWS
    odd = flags_ref[0] == 1
    heads = step_ref.shape[0]
    reach = 3
    count = sums_ref.shape[1]
    per_step = heads // count
    width = values_ref.shape[2]
    groups = coupled_ref.shape[2] // (2 * N)
    share = width // groups
    held = slots * CH

    work = []
    for g in range(groups):
        work.append((coupling_ref, coupled_ref, taps_refs[1::2], g))
        for piece in range(share // WIDE):
            work.append((value_ref, values_ref, taps_refs[0::2], g * (share // WIDE) + piece))
    fill_rows(rows_scr, sources, flags_ref[1], flip)
    later = flags_ref[2] > 0
    tail = jnp.where(later, tail_ref[...].astype(f32), 0.0)
    tail = jnp.concatenate([tail[0:TAIL], tail[TAIL:TAILS]], axis=1)
    tails = [pltpu.roll(tail, TAIL // 2, 0), tail]
    if slots == 1:
        tails = [jnp.where(flags_ref[1] == flip, *tails)] * 2
    rows_scr[held : held + TAILS] = jnp.concatenate(tails).astype(bf16)
    for s, tail in enumerate(tails[:slots]):
        facts(rows_ref, s, ids_row(flags_ref, segments_ref, streams[s]), tail[4:5, 0:CH], reach)
    masks = [turned(rows_ref[s]) for s in range(slots)]
    rows = rows_scr[...]
    step_rows = lax.dot_general(
        step_ref[...], rows_scr[0:held], (((1,), (1,)), ((), ())), preferred_element_type=f32
    )

    def convolved(projected, out_ref, taps_and_shift, at, slot):
        projected = projected.astype(bf16).astype(f32)
        taps, shift = (ref[:, at * WIDE : (at + 1) * WIDE].astype(f32) for ref in taps_and_shift)
        for s in range(slots):
            body = projected[CH * s : CH * (s + 1)]
            start = held + TAIL * s
            pad_scr[slot, s, 0:TAIL] = projected[start : start + TAIL]
            pad_scr[slot, s, TAIL : TAIL + CH] = body
            running = shift + taps[reach : reach + 1] * body
            for k in range(reach):
                window = pad_scr[slot, s, TAIL - reach + k : TAIL - reach + k + CH]
                running = running + taps[k : k + 1] * window * masks[s][:, k : k + 1]
            out_ref[s, :, at * WIDE : (at + 1) * WIDE] = jax.nn.silu(running).astype(bf16)

    source = lax.broadcasted_iota(jnp.int32, (CH, CH), 0)
    position = lax.broadcasted_iota(jnp.int32, (CH, CH), 1)
    upto = (source <= position).astype(f32)

    def put_states(parts, first, columns):
        if carried == 1:
            state_refs[0][first : first + parts[0].shape[0], columns] = parts[0].astype(bf16)
            return
        given = jnp.where(odd, parts[1], parts[0]).astype(bf16)
        kept = jnp.where(odd, parts[0], parts[1]).astype(bf16)
        for ref, part in zip(state_refs, (given, kept)):
            ref[first : first + part.shape[0], columns] = part

    def weighed(s):
        sizes = jax.nn.softplus(
            step_rows[:, s * CH : (s + 1) * CH].astype(bf16).astype(f32) + head_ref[0]
        )
        decays = -sizes * jnp.exp(head_ref[1])
        cumulative = jnp.dot(decays, upto, precision=highest, preferred_element_type=f32)
        last = cumulative[:, CH - 1 : CH]
        kept, ending = rows_ref[s, 4:5], rows_ref[s, 5:6]
        tail_weight = ending * jnp.exp(last - cumulative) * sizes
        growth = kept * jnp.exp(cumulative)
        gap = jnp.zeros((8 - per_step, CH), f32)
        spaced_tail, spaced_growth = [], []
        for jj in range(count):
            own = slice(jj * per_step, (jj + 1) * per_step)
            sums_ref[s, jj, 0:per_step] = cumulative[own]
            sums_ref[s, jj, per_step : 2 * per_step] = sizes[own]
            spaced_tail += [tail_weight[own], gap]
            spaced_growth += [growth[own], gap]
        leading = spread_heads(
            turned(jnp.concatenate(spaced_growth, axis=0))[CH - 8 : CH], per_step, count
        )[7:8]
        coarse = leading.astype(bf16).astype(f32)
        line = lax.broadcasted_iota(jnp.int32, (FACTOR_ROWS, width), 0)
        factor = jnp.where(line == 0, coarse, jnp.where(line == 1, leading - coarse, 0.0))
        return turned(jnp.concatenate(spaced_tail, axis=0)), factor

    def ended(g):
        own = slice(g * share, (g + 1) * share)
        parts = []
        for s in range(slots):
            part = spread_heads(
                weights[s][0][:, g * 8 * count // groups : (g + 1) * 8 * count // groups],
                per_step,
                count // groups,
            )
            weighted = (part * values_ref[s, :, own].astype(f32)).astype(bf16)
            keys = coupled_ref[s, :, g * 2 * N : g * 2 * N + N]
            parts.append(
                lax.dot_general(
                    keys, weighted, (((0,), (0,)), ((), ())), preferred_element_type=f32
                )
            )
        if slots < carried:
            parts = [parts[0][:lines], parts[0][lines:]]
        put_states(parts, 0, own)

    weights = [weighed(s) for s in range(slots)]
    put_states([weights[0][1], weights[-1][1]], lines, slice(0, width))
    per_group = len(work) // groups
    waiting = None
    for i in range(len(work) + 1):
        following = None
        if i < len(work):
            weight_ref, out_ref, taps_and_shift, at = work[i]
            following = (
                dot(rows, weight_ref[:, at * WIDE : (at + 1) * WIDE]),
                out_ref,
                taps_and_shift,
                at,
                i % 2,
            )
        if waiting is not None:
            convolved(*waiting)
            if i % per_group == 0:
                ended(i // per_group - 1)
        waiting = following


def scan_kernel(slots, flip, flags_ref, *refs):
    sources, refs = refs[:2], refs[2:]
    (
        rows_ref,
        gate_ref,
        values_ref,
        coupled_ref,
        sums_ref,
        skip_ref,
        gates_ref,
        local_ref,
        rows_scr,
    ) = refs
    count = sums_ref.shape[1]
    groups = coupled_ref.shape[2] // (2 * N)
    per_step = WIDE // P_SIZE
    fill_rows(rows_scr, sources, flags_ref[1], flip)
    rows = rows_scr[...]
    position = lax.broadcasted_iota(jnp.int32, (CH, CH), 0)
    source = lax.broadcasted_iota(jnp.int32, (CH, CH), 1)
    lane = lax.broadcasted_iota(jnp.int32, (CH, 2 * P_SIZE), 1)
    hidden = []
    for s in range(slots):
        ids = turned(rows_ref[s])[:, 3:4]
        visible = jnp.logical_and(ids == rows_ref[s, 3:4], position >= source)
        hidden.append(jnp.where(visible, 0.0, -1e30))
    scores = None
    for j in range(count):
        if j % (count // groups) == 0:
            g = j // (count // groups)
            scores = [
                lax.dot_general(
                    coupled_ref[s, :, g * 2 * N + N : (g + 1) * 2 * N],
                    coupled_ref[s, :, g * 2 * N : g * 2 * N + N],
                    (((1,), (1,)), ((), ())),
                    preferred_element_type=f32,
                )
                for s in range(slots)
            ]
        for s in range(slots):
            columns = turned(sums_ref[s, j])
            for pair in range(per_step // 2):
                mixing = []
                for h in (2 * pair, 2 * pair + 1):
                    damping = jnp.exp(
                        columns[:, h : h + 1] - sums_ref[s, j, h : h + 1] + hidden[s]
                    )
                    sizes = sums_ref[s, j, per_step + h : per_step + h + 1]
                    mixing.append((scores[s] * damping * sizes).astype(bf16))
                own = slice(j * WIDE + pair * 2 * P_SIZE, j * WIDE + (pair + 1) * 2 * P_SIZE)
                both = values_ref[s, :, own]
                mixed = dot(jnp.concatenate(mixing, axis=0), both)
                local_ref[s, :, own] = (
                    jnp.where(lane < P_SIZE, mixed[0:CH], mixed[CH : 2 * CH])
                    + per_head(skip_ref[...], j * per_step + 2 * pair, 2) * both.astype(f32)
                )
        own = slice(j * WIDE, (j + 1) * WIDE)
        projected = dot(rows, gate_ref[:, own]).astype(bf16)
        for s in range(slots):
            gates_ref[s, :, own] = projected[s * CH : (s + 1) * CH]


def unpacked(block):
    tail = block[block.shape[0] - FACTOR_ROWS :]
    return block[: block.shape[0] - FACTOR_ROWS], tail[0:1] + tail[1:2]


def paired(odd, mine_ref, got_ref):
    mine, got = mine_ref[...].astype(f32), got_ref[...].astype(f32)
    return unpacked(jnp.where(odd, got, mine)), unpacked(jnp.where(odd, mine, got))


def put_packed(out_ref, state, factor):
    lines = state.shape[0]
    out_ref[0:lines] = state.astype(bf16)
    if out_ref.shape[0] > lines:
        coarse = factor.astype(bf16).astype(f32)
        line = lax.broadcasted_iota(jnp.int32, (FACTOR_ROWS, state.shape[1]), 0)
        out_ref[lines : lines + FACTOR_ROWS] = jnp.where(
            line == 0, coarse, jnp.where(line == 1, factor - coarse, 0.0)
        ).astype(bf16)


def join_kernel(flags_ref, mine_ref, got_ref, out_ref):
    even, later = paired(flags_ref[0] == 1, mine_ref, got_ref)
    put_packed(out_ref, later[0] + later[1] * even[0], later[1] * even[1])


def chain_kernel(distance, flags_ref, mine_ref, got_ref, out_ref):
    state, factor = unpacked(mine_ref[...].astype(f32))
    earlier, leading = unpacked(got_ref[...].astype(f32))
    reached = jnp.where(flags_ref[2] >= distance, factor, 0.0)
    put_packed(out_ref, state + reached * earlier, reached * leading)


def finish_kernel(flags_ref, mine_ref, got_ref, before_ref, own_ref, *other_refs):
    odd = flags_ref[0] == 1
    even, _ = paired(odd, mine_ref, got_ref)
    before = jnp.where(flags_ref[2] >= 2, before_ref[...].astype(f32), 0.0)
    between = even[0] + even[1] * before
    own_ref[...] = jnp.where(odd, between, before).astype(bf16)
    for other_ref in other_refs:
        other_ref[...] = jnp.where(odd, before, between).astype(bf16)


def out_kernel(slots, blocks, carried, flags_ref, *refs):
    entry_refs, refs = refs[:carried], refs[carried:]
    (
        local_ref,
        gates_ref,
        coupled_ref,
        sums_ref,
        rows_ref,
        gain_ref,
        out_ref,
        *refs,
    ) = refs
    pieces = 1 if slots == 2 else PIECES
    (
        first_ref,
        *second_refs,
        normed_scr,
    ) = refs[-(2 + pieces) :]
    wide = out_ref.shape[1] // blocks
    odd = flags_ref[0] == 1
    groups = coupled_ref.shape[2] // (2 * N)
    share = local_ref.shape[2] // groups
    count = sums_ref.shape[1]
    per_step = WIDE // P_SIZE
    entries = [entry_refs[0][...]]
    if carried == 2:
        own, other = [ref[...].astype(f32) for ref in entry_refs]
        entries = [jnp.where(odd, a, b).astype(bf16) for a, b in ((own, other), (other, own))]
        if slots == 1:
            entries = [jnp.concatenate(entries)]
    for s in range(slots):
        sums = jnp.concatenate([sums_ref[s, jj] for jj in range(count)], axis=0)
        line = lax.broadcasted_iota(jnp.int32, sums.shape, 0) % 8
        growth = rows_ref[s, 4:5] * jnp.exp(jnp.where(line < per_step, sums, 0.0))
        spread = spread_heads(turned(growth), per_step, count)
        for g in range(groups):
            own = slice(g * share, (g + 1) * share)
            queries = coupled_ref[s, :, g * 2 * N + N : (g + 1) * 2 * N]
            carried = dot(queries, entries[s][:, own])
            scanned = local_ref[s, :, own] + spread[:, own] * carried
            gated = scanned * jax.nn.silu(gates_ref[s, :, own].astype(f32))
            scale = lax.rsqrt(jnp.mean(gated * gated, axis=-1, keepdims=True) + epsilon)
            normed_scr[s * CH : (s + 1) * CH, own] = (gated * scale * gain_ref[:, own]).astype(
                bf16
            )

    normed = normed_scr[...]
    low = flags_ref[1] == 0
    for j in range(blocks):
        own = slice(j * wide, (j + 1) * wide)
        branch = dot(normed, out_ref[:, own])
        if slots == 2:
            first_ref[:, own] = branch[0:CH].astype(bf16)
            second_refs[0][:, own] = branch[CH : 2 * CH].astype(bf16)
        else:
            upper, lower = branch[0:HALF], branch[HALF:CH]
            first_ref[:, own] = jnp.where(low, upper, lower).astype(bf16)
            per_piece = blocks // len(second_refs)
            at = j % per_piece
            second_refs[j // per_piece][:, at * wide : (at + 1) * wide] = jnp.where(
                low, lower, upper
            ).astype(bf16)


def summed(refs):
    return sum(ref[...].astype(f32) for ref in refs)


def add_kernel(pieces, flags_ref, mine_ref, *refs):
    del flags_ref
    other_refs, out_ref = refs[:pieces], refs[-1]
    wide = out_ref.shape[1] // len(other_refs)
    for j, ref in enumerate(other_refs):
        own = slice(j * wide, (j + 1) * wide)
        out_ref[:, own] = (mine_ref[:, own].astype(f32) + ref[...].astype(f32)).astype(bf16)


def give_kernel(flags_ref, *refs):
    *back, out_ref = refs
    chips = len(back) // 2
    out_ref[...] = jnp.where(
        flags_ref[1] == 0, summed(back[chips:]), summed(back[:chips])
    ).astype(bf16)


def close_kernel(flags_ref, rezero_ref, own_ref, mine_ref, others_ref, theirs_ref, *refs):
    *back, out_ref = refs
    chips = len(back) // 2
    core = flags_ref[1]
    ours = jnp.where(core == 0, summed(back[:chips]), summed(back[chips:]))
    for at, far in ((core, ours), (1 - core, theirs_ref[...].astype(f32))):
        lines = pl.ds(pl.multiple_of(at * HALF, HALF), HALF)
        branch = mine_ref[lines].astype(f32) + others_ref[lines].astype(f32) + far
        out_ref[lines] = (own_ref[lines].astype(f32) + rezero_ref[0] * branch).astype(bf16)


IN_VMEM = pl.BlockSpec(memory_space=pltpu.VMEM)
IN_SMEM = pl.BlockSpec(memory_space=pltpu.SMEM)
FLOPS_PER_US = 1_150_000_000


class Sequence:
    def __init__(self, flags):
        self.flags, self.token = flags, None

    def run(self, kernel, name, shapes, scratch, *operands, mib=2, us=1, scalars=()):
        tokens = [] if self.token is None else [self.token]
        given = 1 + len(scalars) + len(operands)

        def ordered(*refs):
            outs = refs[given + len(tokens) :]
            mark_ref = outs[len(shapes)]
            mark_ref[...] = jnp.zeros_like(mark_ref)
            kernel(*refs[:given], *outs[: len(shapes)], *outs[len(shapes) + 1 :])

        *results, self.token = pl.pallas_call(
            ordered,
            in_specs=[IN_SMEM] * (1 + len(scalars)) + [IN_VMEM] * (len(operands) + len(tokens)),
            out_specs=[IN_VMEM] * (len(shapes) + 1),
            out_shape=[*shapes, shape(f32, 8, CH)],
            scratch_shapes=scratch,
            compiler_params=pltpu.CompilerParams(vmem_limit_bytes=mib << 20),
            cost_estimate=pl.CostEstimate(
                flops=int(us * FLOPS_PER_US), bytes_accessed=0, transcendentals=0
            ),
            name=name,
        )(self.flags, *scalars, *operands, *tokens)
        return results

    def held(self, block):
        def hold(block_ref, token_ref, out_ref):
            del block_ref, token_ref, out_ref

        return pl.pallas_call(
            hold,
            in_specs=[IN_VMEM] * 2,
            out_specs=IN_VMEM,
            out_shape=shape(block.dtype, *block.shape),
            input_output_aliases={0: 0},
            compiler_params=pltpu.CompilerParams(vmem_limit_bytes=1 << 20),
            name="hold",
        )(block, self.token)


def shape(dtype, *sizes):
    return jax.ShapeDtypeStruct(sizes, dtype)


def mix(run, slots, streams, flip, carried, sources, tails, segments, weights, small):
    value_weight, coupling_weight = weights
    width, narrow, depth = value_weight.shape[1], coupling_weight.shape[1], value_weight.shape[0]
    shapes = [
        shape(bf16, slots, CH, width),
        shape(bf16, slots, CH, narrow),
        shape(f32, slots, narrow // N, 8, CH),
        shape(f32, slots, 8, CH),
    ] + [shape(bf16, N * slots // carried + FACTOR_ROWS, width)] * carried
    scratch = [
        pltpu.VMEM((slots * CH + TAILS, depth), bf16),
        pltpu.VMEM((2, slots, CH + TAIL, WIDE), f32),
    ]
    kernel = functools.partial(mix_kernel, slots, streams, flip, carried)
    operands = (*sources, *tails, segments, *weights, *small)
    return run(kernel, f"mix{slots}", shapes, scratch, *operands, mib=8, us=4 * slots)


def scan(run, slots, flip, sources, rows, gate_weight, values, coupled, sums, skip):
    shapes = [shape(bf16, *values.shape), shape(f32, *values.shape)]
    scratch = [pltpu.VMEM((slots * CH, gate_weight.shape[0]), bf16)]
    kernel = functools.partial(scan_kernel, slots, flip)
    operands = (*sources, rows, gate_weight, values, coupled, sums, skip)
    return run(kernel, f"scan{slots}", shapes, scratch, *operands, mib=6, us=0.1)


def project_out(run, slots, entries, local, gates, coupled, sums, rows, gain, out_weight, *waits):
    width, depth = out_weight.shape
    lines = CH if slots == 2 else HALF
    scratch = [pltpu.VMEM((slots * CH, width), bf16)]
    kernel = functools.partial(out_kernel, slots, 8, len(entries))
    operands = (*entries, local, gates, coupled, sums, rows, gain, out_weight, *waits)
    pieces = 1 if slots == 2 else PIECES
    shapes = [shape(bf16, lines, depth)] + [shape(bf16, lines, depth // pieces)] * pieces
    return run(kernel, f"out{slots}", shapes, scratch, *operands, mib=6, us=0.1)


def along(block, distance):
    spans = lax.axis_size("ctx")
    return lax.ppermute(block, "ctx", [(i, (i + distance) % spans) for i in range(spans)])


def tail_from(block, chips_on):
    places, spans = lax.axis_size("fsdp"), lax.axis_size("ctx")
    route = [
        ((f + 2 * chips_on) % places * spans + c, f * spans + (c + 1) % spans)
        for f in range(places)
        for c in range(spans)
    ]
    return lax.ppermute(block, ("fsdp", "ctx"), route)


def partner(block, axis):
    return lax.ppermute(block, axis, [(i, i ^ 1) for i in range(lax.axis_size(axis))])


def over(block, distance):
    size = lax.axis_size("fsdp")
    return lax.ppermute(block, "fsdp", [(i, (i + 2 * distance) % size) for i in range(size)])


def joined(run, mine, got):
    return run(join_kernel, "join", [shape(bf16, *mine.shape)], [], mine, got, us=0.1)[0]


def chained(run, block):
    spans = lax.axis_size("ctx")
    lines, width = block.shape
    distance = 2
    while distance < spans // 2:
        last = 2 * distance >= spans // 2
        out = [shape(bf16, lines - FACTOR_ROWS if last else lines, width)]
        kernel = functools.partial(chain_kernel, distance)
        block = run(kernel, "chain", out, [], block, along(block, distance), us=0.1)[0]
        distance *= 2
    return block


def finished(run, kept, got, before, carried):
    out = [shape(bf16, *before.shape)] * carried
    own, *others = run(finish_kernel, "finish", out, [], kept, got, before, us=0.1)
    return own, *[partner(other, "ctx") for other in others]


def on_device(
    tokens,
    segments,
    gate_weight,
    value_weight,
    coupling_weight,
    step_weight,
    value_conv,
    coupling_conv,
    value_shift,
    coupling_shift,
    step_bias,
    decay_log,
    skip_gain,
    norm_gain,
    out_weight,
    rezero,
):
    place = lax.axis_index("fsdp")
    span = lax.axis_index("ctx")
    chips = lax.axis_size("fsdp") // 2
    chip, core = place // 2, place % 2
    own = tokens[0]
    phases = [(d, j) for d in range(1, chips) for j in range(2)]
    far_streams = [(chip + d) % chips * 2 + j for d, j in phases]
    flags = jnp.stack([span % 2, core, span, place, place ^ 1] + far_streams).astype(jnp.int32)

    sequence = Sequence(flags)
    run = sequence.run

    arrived = {d: over(own, -d) for d in range(1, chips)}
    opposite = partner(own, "fsdp")
    half_shape = shape(bf16, HALF, own.shape[1])
    tail_shape = shape(bf16, TAILS, own.shape[1] // 2)
    tail = run(tail_kernel, "tail", [tail_shape], [], own, opposite, segments, us=8)[0]

    heads = step_weight.shape[1]
    head = jnp.broadcast_to(jnp.stack([step_bias, decay_log])[:, :, None], (2, heads, CH))
    skip = skip_gain[None]
    shifts = (value_shift[None], coupling_shift[None])
    small = (step_weight.T, value_conv, coupling_conv, *shifts, head)
    gain = norm_gain[None]

    weights = (value_weight, coupling_weight)
    near = tail_from(tail, 0)
    far = [tail_from(tail, d) for d in range(1, chips)]
    near_sources = (own, opposite)
    values, coupled, near_sums, near_rows, given, near_kept = mix(
        run, 2, (3, 4), None, 2, near_sources, [near, *far], segments, weights, small
    )
    near_mixed = (values, coupled, near_sums)
    near_got = partner(given, "ctx")

    far_mixed = []
    for i, (d, j) in enumerate(phases):
        if j == 0:
            arrival = sequence.held(arrived[d])
            sources = (arrival, partner(arrival, "fsdp"))
        carried = 1
        mixed = mix(
            run, 1, (5 + i,), j, carried, sources, far[d - 1 : d], segments, weights, small
        )
        given, kept = mixed[4], mixed[-1]
        far_mixed.append((sources, *mixed[:4], kept, partner(given, "ctx"), carried))
        if i == 0:
            near_block = joined(run, near_kept, near_got)

    far_scans, blocks, befores = [], [], []
    for i, ((d, j), far_one) in enumerate(zip(phases, far_mixed)):
        sources, values, coupled, sums, rows, kept, got, _ = far_one
        blocks.append(joined(run, kept, got))
        if i == 0:
            near_before = along(chained(run, near_block), 2)
        if i == 1:
            befores.append(along(chained(run, blocks[0]), 2))
        far_scans.append(
            scan(run, 1, j, sources, rows, gate_weight, values, coupled, sums, skip)
        )

    back, latest = {}, ()
    for i, ((d, j), (gates, local), far_one) in enumerate(zip(phases, far_scans, far_mixed)):
        _, _, coupled, sums, rows, kept, got, carried = far_one
        entries = finished(run, kept, got, befores[i], carried)
        mine, *pieces = project_out(
            run,
            1,
            entries,
            local,
            gates,
            coupled,
            sums,
            rows,
            gain,
            out_weight,
            *(near_entries[1:] if i == 1 else ()),
        )
        pieces = [partner(piece, "fsdp") for piece in pieces]
        if i == 0:
            near_entries = finished(run, near_kept, near_got, near_before, 2)
        kernel = functools.partial(add_kernel, len(pieces))
        total = run(kernel, "add", [half_shape], [], mine, *pieces, *latest, us=0.1)[0]
        back[d, j] = over(total, d)
        latest = (back[d, j],)
        if i == 0:
            befores += [along(chained(run, block), 2) for block in blocks[1:]]
            near_gates, near_local = scan(
                run, 2, None, near_sources, near_rows, gate_weight, *near_mixed, skip
            )

    near_mine, near_others = project_out(
        run,
        2,
        near_entries,
        near_local,
        near_gates,
        near_mixed[1],
        near_sums,
        near_rows,
        gain,
        out_weight,
    )
    near_others = partner(near_others, "fsdp")
    returned = [back[d, j] for j in range(2) for d in range(1, chips)]
    given = run(give_kernel, "give", [half_shape], [], *returned, us=0.1)[0]
    return run(
        close_kernel,
        "close",
        [shape(bf16, *own.shape)],
        [],
        own,
        near_mine,
        near_others,
        partner(given, "fsdp"),
        *returned,
        mib=4,
        scalars=(rezero,),
    )[0][None]


def solution(mesh):
    return jax.shard_map(
        on_device,
        mesh=mesh,
        in_specs=(
            P("fsdp", "ctx", None),
            P(None, "ctx"),
            P(None, "fsdp"),
            P(None, "fsdp"),
            P(None, "fsdp"),
            P(None, "fsdp"),
            P(None, "fsdp"),
            P(None, "fsdp"),
            P("fsdp"),
            P("fsdp"),
            P("fsdp"),
            P("fsdp"),
            P("fsdp"),
            P("fsdp"),
            P("fsdp", None),
            P(),
        ),
        out_specs=P("fsdp", "ctx", None),
        check_vma=False,
    )
```

```python
import functools

import jax
import jax.numpy as jnp
from jax import lax
from jax.experimental import pallas as pl
from jax.experimental.pallas import tpu as pltpu
from jax.sharding import PartitionSpec as P

P_SIZE = 64
N = 128
CH = 128
HALF = CH // 2
TAIL = 8
TAILS = 16
WIDE = 256
PIECES = 4
FACTOR_ROWS = 16

epsilon = 1e-05
highest = lax.Precision.HIGHEST
f32 = jnp.float32
bf16 = jnp.bfloat16


def dot(a, b):
    return jnp.dot(a, b, preferred_element_type=f32)


def turned(rows):
    fill = jnp.zeros((N - rows.shape[0], rows.shape[1]), f32)
    return jnp.concatenate([rows, fill], axis=0).T


def per_head(columns, first, heads):
    lane = lax.broadcasted_iota(jnp.int32, (columns.shape[0], 2 * P_SIZE), 1)
    low = lane < P_SIZE
    blocks = [
        jnp.where(low, columns[:, c : c + 1], columns[:, c + 1 : c + 2])
        for c in range(first, first + heads, 2)
    ]
    return jnp.concatenate(blocks, axis=1)


def spread_heads(columns, heads_per_step, steps):
    return jnp.concatenate(
        [per_head(columns, 8 * j, heads_per_step) for j in range(steps)], axis=1
    )


def fill_rows(rows_scr, sources, core, flip):
    if flip is None:
        rows_scr[0:CH] = sources[0][...]
        rows_scr[CH : 2 * CH] = sources[1][...]
        return
    for ref, taken in zip(sources, (core == flip, core != flip)):

        @pl.when(taken)
        def _(ref=ref):
            rows_scr[0:CH] = ref[...]


def ids_row(flags_ref, segments_ref, at):
    ids = segments_ref[...].astype(f32)
    line = lax.broadcasted_iota(jnp.int32, ids.shape, 0)
    return jnp.sum(jnp.where(line == flags_ref[at], ids, 0.0), axis=0, keepdims=True)


def tail_kernel(flags_ref, own_ref, opposite_ref, segments_ref, tail_ref):
    half = tail_ref.shape[1]
    own, opposite = (
        ref[CH - TAILS : CH].astype(f32)[TAILS - TAIL :] for ref in (own_ref, opposite_ref)
    )
    line = lax.broadcasted_iota(jnp.int32, own.shape, 0)
    both = jnp.where(line < TAIL // 2, pltpu.roll(own, TAIL // 2, 0), opposite)
    line = line[:, 0:CH]
    labelled = jnp.where(
        line == 0,
        ids_row(flags_ref, segments_ref, 3),
        jnp.where(line == TAIL // 2, ids_row(flags_ref, segments_ref, 4), both[:, 0:CH]),
    )
    both = jnp.concatenate([labelled, both[:, CH:]], axis=1)
    tail_ref[...] = jnp.concatenate([both[:, :half], both[:, half:]]).astype(bf16)


def facts(rows_ref, s, ids, prior, reach):
    lane = lax.broadcasted_iota(jnp.int32, (8, CH), 1)
    line = lax.broadcasted_iota(jnp.int32, (8, CH), 0)
    ids, prior = (jnp.broadcast_to(a, (8, CH)) for a in (ids, prior))
    found = jnp.zeros((8, CH), f32)
    for k in range(reach):
        back = reach - k
        earlier = jnp.where(lane < back, pltpu.roll(prior, back, 1), pltpu.roll(ids, back, 1))
        found = jnp.where(line == k, jnp.where(earlier == ids, 1.0, 0.0), found)
    found = jnp.where(line == 3, ids, found)
    found = jnp.where(line == 4, jnp.where(ids == prior[:, CH - 1 : CH], 1.0, 0.0), found)
    found = jnp.where(line == 5, jnp.where(ids == ids[:, CH - 1 : CH], 1.0, 0.0), found)
    rows_ref[s] = found


def mix_kernel(slots, streams, flip, flags_ref, *refs):
    sources, refs = refs[:2], refs[2:]
    tail_ref, refs = refs[0], refs[-15 - slots :]
    segments_ref, value_ref, coupling_ref, step_ref, *taps_refs, head_ref = refs[:9]
    refs = refs[9:]
    values_ref, coupled_ref, sums_ref, rows_ref = refs[:4]
    state_refs, (rows_scr, pad_scr) = refs[4 : 4 + slots], refs[4 + slots :]
    odd = flags_ref[0] == 1
    heads = step_ref.shape[0]
    reach = 3
    count = sums_ref.shape[1]
    per_step = heads // count
    width = values_ref.shape[2]
    groups = coupled_ref.shape[2] // (2 * N)
    share = width // groups
    held = slots * CH

    work = []
    for g in range(groups):
        work.append((coupling_ref, coupled_ref, taps_refs[1::2], g))
        for piece in range(share // WIDE):
            work.append((value_ref, values_ref, taps_refs[0::2], g * (share // WIDE) + piece))
    fill_rows(rows_scr, sources, flags_ref[1], flip)
    later = flags_ref[2] > 0
    tail = jnp.where(later, tail_ref[...].astype(f32), 0.0)
    tail = jnp.concatenate([tail[0:TAIL], tail[TAIL:TAILS]], axis=1)
    tails = [pltpu.roll(tail, TAIL // 2, 0), tail]
    if slots == 1:
        tails = [jnp.where(flags_ref[1] == flip, *tails)] * 2
    rows_scr[held : held + TAILS] = jnp.concatenate(tails).astype(bf16)
    for s, tail in enumerate(tails[:slots]):
        facts(rows_ref, s, ids_row(flags_ref, segments_ref, streams[s]), tail[4:5, 0:CH], reach)
    masks = [turned(rows_ref[s]) for s in range(slots)]
    rows = rows_scr[...]
    step_rows = lax.dot_general(
        step_ref[...], rows_scr[0:held], (((1,), (1,)), ((), ())), preferred_element_type=f32
    )

    def convolved(projected, out_ref, taps_and_shift, at, slot):
        projected = projected.astype(bf16).astype(f32)
        taps, shift = (ref[:, at * WIDE : (at + 1) * WIDE].astype(f32) for ref in taps_and_shift)
        for s in range(slots):
            body = projected[CH * s : CH * (s + 1)]
            start = held + TAIL * s
            pad_scr[slot, s, 0:TAIL] = projected[start : start + TAIL]
            pad_scr[slot, s, TAIL : TAIL + CH] = body
            running = shift + taps[reach : reach + 1] * body
            for k in range(reach):
                window = pad_scr[slot, s, TAIL - reach + k : TAIL - reach + k + CH]
                running = running + taps[k : k + 1] * window * masks[s][:, k : k + 1]
            out_ref[s, :, at * WIDE : (at + 1) * WIDE] = jax.nn.silu(running).astype(bf16)

    source = lax.broadcasted_iota(jnp.int32, (CH, CH), 0)
    position = lax.broadcasted_iota(jnp.int32, (CH, CH), 1)
    upto = (source <= position).astype(f32)

    def put_states(parts, first, columns):
        if slots == 1:
            state_refs[0][first : first + parts[0].shape[0], columns] = parts[0].astype(bf16)
            return
        given = jnp.where(odd, parts[1], parts[0]).astype(bf16)
        kept = jnp.where(odd, parts[0], parts[1]).astype(bf16)
        for ref, part in zip(state_refs, (given, kept)):
            ref[first : first + part.shape[0], columns] = part

    def weighed(s):
        sizes = jax.nn.softplus(
            step_rows[:, s * CH : (s + 1) * CH].astype(bf16).astype(f32) + head_ref[0]
        )
        decays = -sizes * jnp.exp(head_ref[1])
        cumulative = jnp.dot(decays, upto, precision=highest, preferred_element_type=f32)
        last = cumulative[:, CH - 1 : CH]
        kept, ending = rows_ref[s, 4:5], rows_ref[s, 5:6]
        tail_weight = ending * jnp.exp(last - cumulative) * sizes
        growth = kept * jnp.exp(cumulative)
        gap = jnp.zeros((8 - per_step, CH), f32)
        spaced_tail, spaced_growth = [], []
        for jj in range(count):
            own = slice(jj * per_step, (jj + 1) * per_step)
            sums_ref[s, jj, 0:per_step] = cumulative[own]
            sums_ref[s, jj, per_step : 2 * per_step] = sizes[own]
            spaced_tail += [tail_weight[own], gap]
            spaced_growth += [growth[own], gap]
        leading = spread_heads(
            turned(jnp.concatenate(spaced_growth, axis=0))[CH - 8 : CH], per_step, count
        )[7:8]
        coarse = leading.astype(bf16).astype(f32)
        line = lax.broadcasted_iota(jnp.int32, (FACTOR_ROWS, width), 0)
        factor = jnp.where(line == 0, coarse, jnp.where(line == 1, leading - coarse, 0.0))
        return turned(jnp.concatenate(spaced_tail, axis=0)), factor

    def ended(g):
        own = slice(g * share, (g + 1) * share)
        parts = []
        for s in range(slots):
            part = spread_heads(
                weights[s][0][:, g * 8 * count // groups : (g + 1) * 8 * count // groups],
                per_step,
                count // groups,
            )
            weighted = (part * values_ref[s, :, own].astype(f32)).astype(bf16)
            keys = coupled_ref[s, :, g * 2 * N : g * 2 * N + N]
            parts.append(
                lax.dot_general(
                    keys, weighted, (((0,), (0,)), ((), ())), preferred_element_type=f32
                )
            )
        put_states(parts, 0, own)

    weights = [weighed(s) for s in range(slots)]
    put_states([w[1] for w in weights], N, slice(0, width))
    per_group = len(work) // groups
    waiting = None
    for i in range(len(work) + 1):
        following = None
        if i < len(work):
            weight_ref, out_ref, taps_and_shift, at = work[i]
            following = (
                dot(rows, weight_ref[:, at * WIDE : (at + 1) * WIDE]),
                out_ref,
                taps_and_shift,
                at,
                i % 2,
            )
        if waiting is not None:
            convolved(*waiting)
            if i % per_group == 0:
                ended(i // per_group - 1)
        waiting = following


def scan_kernel(slots, flip, flags_ref, *refs):
    sources, refs = refs[:2], refs[2:]
    (
        rows_ref,
        gate_ref,
        values_ref,
        coupled_ref,
        sums_ref,
        skip_ref,
        gates_ref,
        local_ref,
        rows_scr,
    ) = refs
    count = sums_ref.shape[1]
    groups = coupled_ref.shape[2] // (2 * N)
    per_step = WIDE // P_SIZE
    fill_rows(rows_scr, sources, flags_ref[1], flip)
    rows = rows_scr[...]
    position = lax.broadcasted_iota(jnp.int32, (CH, CH), 0)
    source = lax.broadcasted_iota(jnp.int32, (CH, CH), 1)
    lane = lax.broadcasted_iota(jnp.int32, (CH, 2 * P_SIZE), 1)
    hidden = []
    for s in range(slots):
        ids = turned(rows_ref[s])[:, 3:4]
        visible = jnp.logical_and(ids == rows_ref[s, 3:4], position >= source)
        hidden.append(jnp.where(visible, 0.0, -1e30))
    scores = None
    for j in range(count):
        if j % (count // groups) == 0:
            g = j // (count // groups)
            scores = [
                lax.dot_general(
                    coupled_ref[s, :, g * 2 * N + N : (g + 1) * 2 * N],
                    coupled_ref[s, :, g * 2 * N : g * 2 * N + N],
                    (((1,), (1,)), ((), ())),
                    preferred_element_type=f32,
                )
                for s in range(slots)
            ]
        for s in range(slots):
            columns = turned(sums_ref[s, j])
            for pair in range(per_step // 2):
                mixing = []
                for h in (2 * pair, 2 * pair + 1):
                    damping = jnp.exp(
                        columns[:, h : h + 1] - sums_ref[s, j, h : h + 1] + hidden[s]
                    )
                    sizes = sums_ref[s, j, per_step + h : per_step + h + 1]
                    mixing.append((scores[s] * damping * sizes).astype(bf16))
                own = slice(j * WIDE + pair * 2 * P_SIZE, j * WIDE + (pair + 1) * 2 * P_SIZE)
                both = values_ref[s, :, own]
                mixed = dot(jnp.concatenate(mixing, axis=0), both)
                local_ref[s, :, own] = (
                    jnp.where(lane < P_SIZE, mixed[0:CH], mixed[CH : 2 * CH])
                    + per_head(skip_ref[...], j * per_step + 2 * pair, 2) * both.astype(f32)
                )
        own = slice(j * WIDE, (j + 1) * WIDE)
        projected = dot(rows, gate_ref[:, own]).astype(bf16)
        for s in range(slots):
            gates_ref[s, :, own] = projected[s * CH : (s + 1) * CH]


def unpacked(block):
    tail = block[block.shape[0] - FACTOR_ROWS :]
    return block[: block.shape[0] - FACTOR_ROWS], tail[0:1] + tail[1:2]


def paired(odd, mine_ref, got_ref):
    mine, got = mine_ref[...].astype(f32), got_ref[...].astype(f32)
    return unpacked(jnp.where(odd, got, mine)), unpacked(jnp.where(odd, mine, got))


def put_packed(out_ref, state, factor):
    lines = state.shape[0]
    out_ref[0:lines] = state.astype(bf16)
    if out_ref.shape[0] > lines:
        coarse = factor.astype(bf16).astype(f32)
        line = lax.broadcasted_iota(jnp.int32, (FACTOR_ROWS, state.shape[1]), 0)
        out_ref[lines : lines + FACTOR_ROWS] = jnp.where(
            line == 0, coarse, jnp.where(line == 1, factor - coarse, 0.0)
        ).astype(bf16)


def join_kernel(flags_ref, mine_ref, got_ref, out_ref):
    even, later = paired(flags_ref[0] == 1, mine_ref, got_ref)
    put_packed(out_ref, later[0] + later[1] * even[0], later[1] * even[1])


def chain_kernel(distance, flags_ref, mine_ref, got_ref, out_ref):
    state, factor = unpacked(mine_ref[...].astype(f32))
    earlier, leading = unpacked(got_ref[...].astype(f32))
    reached = jnp.where(flags_ref[2] >= distance, factor, 0.0)
    put_packed(out_ref, state + reached * earlier, reached * leading)


def entered(flags_ref, mine_ref, got_ref, before_ref):
    odd = flags_ref[0] == 1
    even, _ = paired(odd, mine_ref, got_ref)
    before = jnp.where(flags_ref[2] >= 2, before_ref[...].astype(f32), 0.0)
    between = even[0] + even[1] * before
    return jnp.where(odd, between, before), jnp.where(odd, before, between)


def finish_kernel(flags_ref, mine_ref, got_ref, before_ref, own_ref, other_ref):
    own, other = entered(flags_ref, mine_ref, got_ref, before_ref)
    own_ref[...] = own.astype(bf16)
    other_ref[...] = other.astype(bf16)


def out_kernel(slots, blocks, flags_ref, *refs):
    entry_refs, refs = refs[: 4 - slots], refs[4 - slots :]
    (
        local_ref,
        gates_ref,
        coupled_ref,
        sums_ref,
        rows_ref,
        gain_ref,
        out_ref,
        *refs,
    ) = refs
    pieces = 1 if slots == 2 else PIECES
    (
        first_ref,
        *second_refs,
        normed_scr,
    ) = refs[-(2 + pieces) :]
    wide = out_ref.shape[1] // blocks
    odd = flags_ref[0] == 1
    groups = coupled_ref.shape[2] // (2 * N)
    share = local_ref.shape[2] // groups
    count = sums_ref.shape[1]
    per_step = WIDE // P_SIZE
    if slots == 1:
        entries = [entered(flags_ref, *entry_refs)[0].astype(bf16)]
    else:
        own, other = [ref[...].astype(f32) for ref in entry_refs]
        entries = [jnp.where(odd, a, b).astype(bf16) for a, b in ((own, other), (other, own))]
    for s in range(slots):
        sums = jnp.concatenate([sums_ref[s, jj] for jj in range(count)], axis=0)
        line = lax.broadcasted_iota(jnp.int32, sums.shape, 0) % 8
        growth = rows_ref[s, 4:5] * jnp.exp(jnp.where(line < per_step, sums, 0.0))
        spread = spread_heads(turned(growth), per_step, count)
        for g in range(groups):
            own = slice(g * share, (g + 1) * share)
            queries = coupled_ref[s, :, g * 2 * N + N : (g + 1) * 2 * N]
            carried = dot(queries, entries[s][:, own])
            scanned = local_ref[s, :, own] + spread[:, own] * carried
            gated = scanned * jax.nn.silu(gates_ref[s, :, own].astype(f32))
            scale = lax.rsqrt(jnp.mean(gated * gated, axis=-1, keepdims=True) + epsilon)
            normed_scr[s * CH : (s + 1) * CH, own] = (gated * scale * gain_ref[:, own]).astype(
                bf16
            )

    normed = normed_scr[...]
    low = flags_ref[1] == 0
    for j in range(blocks):
        own = slice(j * wide, (j + 1) * wide)
        branch = dot(normed, out_ref[:, own])
        if slots == 2:
            first_ref[:, own] = branch[0:CH].astype(bf16)
            second_refs[0][:, own] = branch[CH : 2 * CH].astype(bf16)
        else:
            upper, lower = branch[0:HALF], branch[HALF:CH]
            first_ref[:, own] = jnp.where(low, upper, lower).astype(bf16)
            per_piece = blocks // len(second_refs)
            at = j % per_piece
            second_refs[j // per_piece][:, at * wide : (at + 1) * wide] = jnp.where(
                low, lower, upper
            ).astype(bf16)


def summed(refs):
    return sum(ref[...].astype(f32) for ref in refs)


def add_kernel(pieces, flags_ref, mine_ref, *refs):
    del flags_ref
    other_refs, out_ref = refs[:pieces], refs[-1]
    wide = out_ref.shape[1] // len(other_refs)
    for j, ref in enumerate(other_refs):
        own = slice(j * wide, (j + 1) * wide)
        out_ref[:, own] = (mine_ref[:, own].astype(f32) + ref[...].astype(f32)).astype(bf16)


def close_kernel(flags_ref, rezero_ref, own_ref, mine_ref, others_ref, *refs):
    *back, out_ref = refs
    chips, core = len(back) // 4, flags_ref[1]
    sums = [back[i * chips : (i + 1) * chips] for i in range(4)]
    ours = jnp.where(core == 0, summed(sums[0]), summed(sums[1]))
    theirs = jnp.where(core == 0, summed(sums[2]), summed(sums[3]))
    for at, far in ((core, ours), (1 - core, theirs)):
        lines = pl.ds(pl.multiple_of(at * HALF, HALF), HALF)
        branch = mine_ref[lines].astype(f32) + others_ref[lines].astype(f32) + far
        out_ref[lines] = (own_ref[lines].astype(f32) + rezero_ref[0] * branch).astype(bf16)


IN_VMEM = pl.BlockSpec(memory_space=pltpu.VMEM)
IN_SMEM = pl.BlockSpec(memory_space=pltpu.SMEM)
FLOPS_PER_US = 1_150_000_000


class Sequence:
    def __init__(self, flags):
        self.flags, self.token = flags, None

    def run(self, kernel, name, shapes, scratch, *operands, mib=2, us=1, scalars=()):
        tokens = [] if self.token is None else [self.token]
        given = 1 + len(scalars) + len(operands)

        def ordered(*refs):
            outs = refs[given + len(tokens) :]
            mark_ref = outs[len(shapes)]
            mark_ref[...] = jnp.zeros_like(mark_ref)
            kernel(*refs[:given], *outs[: len(shapes)], *outs[len(shapes) + 1 :])

        *results, self.token = pl.pallas_call(
            ordered,
            in_specs=[IN_SMEM] * (1 + len(scalars)) + [IN_VMEM] * (len(operands) + len(tokens)),
            out_specs=[IN_VMEM] * (len(shapes) + 1),
            out_shape=[*shapes, shape(f32, 8, CH)],
            scratch_shapes=scratch,
            compiler_params=pltpu.CompilerParams(vmem_limit_bytes=mib << 20),
            cost_estimate=pl.CostEstimate(
                flops=int(us * FLOPS_PER_US), bytes_accessed=0, transcendentals=0
            ),
            name=name,
        )(self.flags, *scalars, *operands, *tokens)
        return results

    def held(self, block):
        def hold(block_ref, token_ref, out_ref):
            del block_ref, token_ref, out_ref

        return pl.pallas_call(
            hold,
            in_specs=[IN_VMEM] * 2,
            out_specs=IN_VMEM,
            out_shape=shape(block.dtype, *block.shape),
            input_output_aliases={0: 0},
            compiler_params=pltpu.CompilerParams(vmem_limit_bytes=1 << 20),
            name="hold",
        )(block, self.token)


def shape(dtype, *sizes):
    return jax.ShapeDtypeStruct(sizes, dtype)


def mix(run, slots, streams, flip, sources, tails, segments, weights, small):
    value_weight, coupling_weight = weights
    width, narrow, depth = value_weight.shape[1], coupling_weight.shape[1], value_weight.shape[0]
    shapes = [
        shape(bf16, slots, CH, width),
        shape(bf16, slots, CH, narrow),
        shape(f32, slots, narrow // N, 8, CH),
        shape(f32, slots, 8, CH),
    ] + [shape(bf16, N + FACTOR_ROWS, width)] * slots
    scratch = [
        pltpu.VMEM((slots * CH + TAILS, depth), bf16),
        pltpu.VMEM((2, slots, CH + TAIL, WIDE), f32),
    ]
    kernel = functools.partial(mix_kernel, slots, streams, flip)
    operands = (*sources, *tails, segments, *weights, *small)
    return run(kernel, f"mix{slots}", shapes, scratch, *operands, mib=8, us=4 * slots)


def scan(run, slots, flip, sources, rows, gate_weight, values, coupled, sums, skip):
    shapes = [shape(bf16, *values.shape), shape(f32, *values.shape)]
    scratch = [pltpu.VMEM((slots * CH, gate_weight.shape[0]), bf16)]
    kernel = functools.partial(scan_kernel, slots, flip)
    operands = (*sources, rows, gate_weight, values, coupled, sums, skip)
    return run(kernel, f"scan{slots}", shapes, scratch, *operands, mib=6, us=0.1)


def project_out(run, slots, entries, local, gates, coupled, sums, rows, gain, out_weight, *waits):
    width, depth = out_weight.shape
    lines = CH if slots == 2 else HALF
    scratch = [pltpu.VMEM((slots * CH, width), bf16)]
    kernel = functools.partial(out_kernel, slots, 8)
    operands = (*entries, local, gates, coupled, sums, rows, gain, out_weight, *waits)
    pieces = 1 if slots == 2 else PIECES
    shapes = [shape(bf16, lines, depth)] + [shape(bf16, lines, depth // pieces)] * pieces
    return run(kernel, f"out{slots}", shapes, scratch, *operands, mib=6, us=0.1)


def along(block, distance):
    spans = lax.axis_size("ctx")
    return lax.ppermute(block, "ctx", [(i, (i + distance) % spans) for i in range(spans)])


def tail_from(block, chips_on):
    places, spans = lax.axis_size("fsdp"), lax.axis_size("ctx")
    route = [
        ((f + 2 * chips_on) % places * spans + c, f * spans + (c + 1) % spans)
        for f in range(places)
        for c in range(spans)
    ]
    return lax.ppermute(block, ("fsdp", "ctx"), route)


def partner(block, axis):
    return lax.ppermute(block, axis, [(i, i ^ 1) for i in range(lax.axis_size(axis))])


def over(block, distance):
    size = lax.axis_size("fsdp")
    return lax.ppermute(block, "fsdp", [(i, (i + 2 * distance) % size) for i in range(size)])


def joined(run, mine, got):
    return run(join_kernel, "join", [shape(bf16, *mine.shape)], [], mine, got, us=0.1)[0]


def chained(run, block):
    spans = lax.axis_size("ctx")
    lines, width = block.shape
    distance = 2
    while distance < spans // 2:
        last = 2 * distance >= spans // 2
        out = [shape(bf16, lines - FACTOR_ROWS if last else lines, width)]
        kernel = functools.partial(chain_kernel, distance)
        block = run(kernel, "chain", out, [], block, along(block, distance), us=0.1)[0]
        distance *= 2
    return block


def finished(run, kept, got, before):
    out = [shape(bf16, *before.shape)] * 2
    own, other = run(finish_kernel, "finish", out, [], kept, got, before, us=0.1)
    return own, partner(other, "ctx")


def on_device(
    tokens,
    segments,
    gate_weight,
    value_weight,
    coupling_weight,
    step_weight,
    value_conv,
    coupling_conv,
    value_shift,
    coupling_shift,
    step_bias,
    decay_log,
    skip_gain,
    norm_gain,
    out_weight,
    rezero,
):
    place = lax.axis_index("fsdp")
    span = lax.axis_index("ctx")
    chips = lax.axis_size("fsdp") // 2
    chip, core = place // 2, place % 2
    own = tokens[0]
    phases = [(d, j) for d in range(1, chips) for j in range(2)]
    far_streams = [(chip + d) % chips * 2 + j for d, j in phases]
    flags = jnp.stack([span % 2, core, span, place, place ^ 1] + far_streams).astype(jnp.int32)

    sequence = Sequence(flags)
    run = sequence.run

    arrived = {d: over(own, -d) for d in range(1, chips)}
    opposite = partner(own, "fsdp")
    half_shape = shape(bf16, HALF, own.shape[1])
    tail_shape = shape(bf16, TAILS, own.shape[1] // 2)
    tail = run(tail_kernel, "tail", [tail_shape], [], own, opposite, segments, us=8)[0]

    heads = step_weight.shape[1]
    head = jnp.broadcast_to(jnp.stack([step_bias, decay_log])[:, :, None], (2, heads, CH))
    skip = skip_gain[None]
    shifts = (value_shift[None], coupling_shift[None])
    small = (step_weight.T, value_conv, coupling_conv, *shifts, head)
    gain = norm_gain[None]

    weights = (value_weight, coupling_weight)
    near = tail_from(tail, 0)
    far = [tail_from(tail, d) for d in range(1, chips)]
    near_sources = (own, opposite)
    values, coupled, near_sums, near_rows, given, near_kept = mix(
        run, 2, (3, 4), None, near_sources, [near, *far], segments, weights, small
    )
    near_mixed = (values, coupled, near_sums)
    near_got = partner(given, "ctx")

    far_mixed = []
    for i, (d, j) in enumerate(phases):
        if j == 0:
            arrival = sequence.held(arrived[d])
            sources = (arrival, partner(arrival, "fsdp"))
        mixed = mix(
            run, 1, (5 + i,), j, sources, far[d - 1 : d], segments, weights, small
        )
        far_mixed.append((sources, *mixed, partner(mixed[-1], "ctx")))
        if i == 0:
            near_block = joined(run, near_kept, near_got)

    far_scans, blocks, befores = [], [], []
    for i, ((d, j), far_one) in enumerate(zip(phases, far_mixed)):
        sources, values, coupled, sums, rows, kept, got = far_one
        blocks.append(joined(run, kept, got))
        if i == 0:
            near_before = along(chained(run, near_block), 2)
        if i == 1:
            befores.append(along(chained(run, blocks[0]), 2))
        far_scans.append(
            scan(run, 1, j, sources, rows, gate_weight, values, coupled, sums, skip)
        )

    back, latest = {}, ()
    for i, ((d, j), (gates, local), far_one) in enumerate(zip(phases, far_scans, far_mixed)):
        _, _, coupled, sums, rows, kept, got = far_one
        mine, *pieces = project_out(
            run,
            1,
            (kept, got, befores[i]),
            local,
            gates,
            coupled,
            sums,
            rows,
            gain,
            out_weight,
            *(near_entries[1:] if i == 1 else ()),
        )
        pieces = [partner(piece, "fsdp") for piece in pieces]
        if i == 0:
            near_entries = finished(run, near_kept, near_got, near_before)
        kernel = functools.partial(add_kernel, len(pieces))
        total = run(kernel, "add", [half_shape], [], mine, *pieces, *latest, us=0.1)[0]
        back[d, j] = over(total, d)
        latest = (back[d, j],)
        if i == 0:
            befores += [along(chained(run, block), 2) for block in blocks[1:]]
            near_gates, near_local = scan(
                run, 2, None, near_sources, near_rows, gate_weight, *near_mixed, skip
            )

    near_mine, near_others = project_out(
        run,
        2,
        near_entries,
        near_local,
        near_gates,
        near_mixed[1],
        near_sums,
        near_rows,
        gain,
        out_weight,
    )
    near_others = partner(near_others, "fsdp")
    returned = [back[d, j] for j in range(2) for d in range(1, chips)]
    return run(
        close_kernel,
        "close",
        [shape(bf16, *own.shape)],
        [],
        own,
        near_mine,
        near_others,
        *returned,
        *[partner(block, "fsdp") for block in returned],
        mib=4,
        scalars=(rezero,),
    )[0][None]


def solution(mesh):
    return jax.shard_map(
        on_device,
        mesh=mesh,
        in_specs=(
            P("fsdp", "ctx", None),
            P(None, "ctx"),
            P(None, "fsdp"),
            P(None, "fsdp"),
            P(None, "fsdp"),
            P(None, "fsdp"),
            P(None, "fsdp"),
            P(None, "fsdp"),
            P("fsdp"),
            P("fsdp"),
            P("fsdp"),
            P("fsdp"),
            P("fsdp"),
            P("fsdp"),
            P("fsdp", None),
            P(),
        ),
        out_specs=P("fsdp", "ctx", None),
        check_vma=False,
    )
```

```python
import functools

import jax
import jax.numpy as jnp
from jax import lax
from jax.experimental import pallas as pl
from jax.experimental.pallas import tpu as pltpu
from jax.sharding import PartitionSpec as P

P_SIZE = 64
N = 128
CH = 128
HALF = CH // 2
TAIL = 8
TAILS = 16
WIDE = 256
PIECES = 2
FACTOR_ROWS = 16

epsilon = 1e-05
highest = lax.Precision.HIGHEST
f32 = jnp.float32
bf16 = jnp.bfloat16


def dot(a, b):
    return jnp.dot(a, b, preferred_element_type=f32)


def turned(rows):
    fill = jnp.zeros((N - rows.shape[0], rows.shape[1]), f32)
    return jnp.concatenate([rows, fill], axis=0).T


def per_head(columns, first, heads):
    lane = lax.broadcasted_iota(jnp.int32, (columns.shape[0], 2 * P_SIZE), 1)
    low = lane < P_SIZE
    blocks = [
        jnp.where(low, columns[:, c : c + 1], columns[:, c + 1 : c + 2])
        for c in range(first, first + heads, 2)
    ]
    return jnp.concatenate(blocks, axis=1)


def spread_heads(columns, heads_per_step, steps):
    return jnp.concatenate(
        [per_head(columns, 8 * j, heads_per_step) for j in range(steps)], axis=1
    )


def fill_rows(rows_scr, sources, core, flip):
    if flip is None:
        rows_scr[0:CH] = sources[0][...]
        rows_scr[CH : 2 * CH] = sources[1][...]
        return
    for ref, taken in zip(sources, (core == flip, core != flip)):

        @pl.when(taken)
        def _(ref=ref):
            rows_scr[0:CH] = ref[...]


def ids_row(flags_ref, segments_ref, at):
    ids = segments_ref[...].astype(f32)
    line = lax.broadcasted_iota(jnp.int32, ids.shape, 0)
    return jnp.sum(jnp.where(line == flags_ref[at], ids, 0.0), axis=0, keepdims=True)


def tail_kernel(flags_ref, own_ref, opposite_ref, segments_ref, tail_ref):
    half = tail_ref.shape[1]
    own, opposite = (
        ref[CH - TAILS : CH].astype(f32)[TAILS - TAIL :] for ref in (own_ref, opposite_ref)
    )
    line = lax.broadcasted_iota(jnp.int32, own.shape, 0)
    both = jnp.where(line < TAIL // 2, pltpu.roll(own, TAIL // 2, 0), opposite)
    line = line[:, 0:CH]
    labelled = jnp.where(
        line == 0,
        ids_row(flags_ref, segments_ref, 3),
        jnp.where(line == TAIL // 2, ids_row(flags_ref, segments_ref, 4), both[:, 0:CH]),
    )
    both = jnp.concatenate([labelled, both[:, CH:]], axis=1)
    tail_ref[...] = jnp.concatenate([both[:, :half], both[:, half:]]).astype(bf16)


def facts(rows_ref, s, ids, prior, reach):
    lane = lax.broadcasted_iota(jnp.int32, (8, CH), 1)
    line = lax.broadcasted_iota(jnp.int32, (8, CH), 0)
    ids, prior = (jnp.broadcast_to(a, (8, CH)) for a in (ids, prior))
    found = jnp.zeros((8, CH), f32)
    for k in range(reach):
        back = reach - k
        earlier = jnp.where(lane < back, pltpu.roll(prior, back, 1), pltpu.roll(ids, back, 1))
        found = jnp.where(line == k, jnp.where(earlier == ids, 1.0, 0.0), found)
    found = jnp.where(line == 3, ids, found)
    found = jnp.where(line == 4, jnp.where(ids == prior[:, CH - 1 : CH], 1.0, 0.0), found)
    found = jnp.where(line == 5, jnp.where(ids == ids[:, CH - 1 : CH], 1.0, 0.0), found)
    rows_ref[s] = found


def mix_kernel(slots, streams, flip, flags_ref, *refs):
    sources, refs = refs[:2], refs[2:]
    tail_ref, refs = refs[0], refs[-15 - slots :]
    segments_ref, value_ref, coupling_ref, step_ref, *taps_refs, head_ref = refs[:9]
    refs = refs[9:]
    values_ref, coupled_ref, sums_ref, rows_ref = refs[:4]
    state_refs, (rows_scr, pad_scr) = refs[4 : 4 + slots], refs[4 + slots :]
    odd = flags_ref[0] == 1
    heads = step_ref.shape[0]
    reach = 3
    count = sums_ref.shape[1]
    per_step = heads // count
    width = values_ref.shape[2]
    groups = coupled_ref.shape[2] // (2 * N)
    share = width // groups
    held = slots * CH

    work = []
    for g in range(groups):
        work.append((coupling_ref, coupled_ref, taps_refs[1::2], g))
        for piece in range(share // WIDE):
            work.append((value_ref, values_ref, taps_refs[0::2], g * (share // WIDE) + piece))
    fill_rows(rows_scr, sources, flags_ref[1], flip)
    later = flags_ref[2] > 0
    tail = jnp.where(later, tail_ref[...].astype(f32), 0.0)
    tail = jnp.concatenate([tail[0:TAIL], tail[TAIL:TAILS]], axis=1)
    tails = [pltpu.roll(tail, TAIL // 2, 0), tail]
    if slots == 1:
        tails = [jnp.where(flags_ref[1] == flip, *tails)] * 2
    rows_scr[held : held + TAILS] = jnp.concatenate(tails).astype(bf16)
    for s, tail in enumerate(tails[:slots]):
        facts(rows_ref, s, ids_row(flags_ref, segments_ref, streams[s]), tail[4:5, 0:CH], reach)
    masks = [turned(rows_ref[s]) for s in range(slots)]
    rows = rows_scr[...]
    step_rows = lax.dot_general(
        step_ref[...], rows_scr[0:held], (((1,), (1,)), ((), ())), preferred_element_type=f32
    )

    def convolved(projected, out_ref, taps_and_shift, at, slot):
        projected = projected.astype(bf16).astype(f32)
        taps, shift = (ref[:, at * WIDE : (at + 1) * WIDE].astype(f32) for ref in taps_and_shift)
        for s in range(slots):
            body = projected[CH * s : CH * (s + 1)]
            start = held + TAIL * s
            pad_scr[slot, s, 0:TAIL] = projected[start : start + TAIL]
            pad_scr[slot, s, TAIL : TAIL + CH] = body
            running = shift + taps[reach : reach + 1] * body
            for k in range(reach):
                window = pad_scr[slot, s, TAIL - reach + k : TAIL - reach + k + CH]
                running = running + taps[k : k + 1] * window * masks[s][:, k : k + 1]
            out_ref[s, :, at * WIDE : (at + 1) * WIDE] = jax.nn.silu(running).astype(bf16)

    source = lax.broadcasted_iota(jnp.int32, (CH, CH), 0)
    position = lax.broadcasted_iota(jnp.int32, (CH, CH), 1)
    upto = (source <= position).astype(f32)

    def put_states(parts, first, columns):
        if slots == 1:
            state_refs[0][first : first + parts[0].shape[0], columns] = parts[0].astype(bf16)
            return
        given = jnp.where(odd, parts[1], parts[0]).astype(bf16)
        kept = jnp.where(odd, parts[0], parts[1]).astype(bf16)
        for ref, part in zip(state_refs, (given, kept)):
            ref[first : first + part.shape[0], columns] = part

    def weighed(s):
        sizes = jax.nn.softplus(
            step_rows[:, s * CH : (s + 1) * CH].astype(bf16).astype(f32) + head_ref[0]
        )
        decays = -sizes * jnp.exp(head_ref[1])
        cumulative = jnp.dot(decays, upto, precision=highest, preferred_element_type=f32)
        last = cumulative[:, CH - 1 : CH]
        kept, ending = rows_ref[s, 4:5], rows_ref[s, 5:6]
        tail_weight = ending * jnp.exp(last - cumulative) * sizes
        growth = kept * jnp.exp(cumulative)
        gap = jnp.zeros((8 - per_step, CH), f32)
        spaced_tail, spaced_growth = [], []
        for jj in range(count):
            own = slice(jj * per_step, (jj + 1) * per_step)
            sums_ref[s, jj, 0:per_step] = cumulative[own]
            sums_ref[s, jj, per_step : 2 * per_step] = sizes[own]
            spaced_tail += [tail_weight[own], gap]
            spaced_growth += [growth[own], gap]
        leading = spread_heads(
            turned(jnp.concatenate(spaced_growth, axis=0))[CH - 8 : CH], per_step, count
        )[7:8]
        coarse = leading.astype(bf16).astype(f32)
        line = lax.broadcasted_iota(jnp.int32, (FACTOR_ROWS, width), 0)
        factor = jnp.where(line == 0, coarse, jnp.where(line == 1, leading - coarse, 0.0))
        return turned(jnp.concatenate(spaced_tail, axis=0)), factor

    def ended(g):
        own = slice(g * share, (g + 1) * share)
        parts = []
        for s in range(slots):
            part = spread_heads(
                weights[s][0][:, g * 8 * count // groups : (g + 1) * 8 * count // groups],
                per_step,
                count // groups,
            )
            weighted = (part * values_ref[s, :, own].astype(f32)).astype(bf16)
            keys = coupled_ref[s, :, g * 2 * N : g * 2 * N + N]
            parts.append(
                lax.dot_general(
                    keys, weighted, (((0,), (0,)), ((), ())), preferred_element_type=f32
                )
            )
        put_states(parts, 0, own)

    weights = [weighed(s) for s in range(slots)]
    put_states([w[1] for w in weights], N, slice(0, width))
    per_group = len(work) // groups
    waiting = None
    for i in range(len(work) + 1):
        following = None
        if i < len(work):
            weight_ref, out_ref, taps_and_shift, at = work[i]
            following = (
                dot(rows, weight_ref[:, at * WIDE : (at + 1) * WIDE]),
                out_ref,
                taps_and_shift,
                at,
                i % 2,
            )
        if waiting is not None:
            convolved(*waiting)
            if i % per_group == 0:
                ended(i // per_group - 1)
        waiting = following


def scan_kernel(slots, flip, flags_ref, *refs):
    sources, refs = refs[:2], refs[2:]
    (
        rows_ref,
        gate_ref,
        values_ref,
        coupled_ref,
        sums_ref,
        skip_ref,
        gates_ref,
        local_ref,
        rows_scr,
    ) = refs
    count = sums_ref.shape[1]
    groups = coupled_ref.shape[2] // (2 * N)
    per_step = WIDE // P_SIZE
    fill_rows(rows_scr, sources, flags_ref[1], flip)
    rows = rows_scr[...]
    position = lax.broadcasted_iota(jnp.int32, (CH, CH), 0)
    source = lax.broadcasted_iota(jnp.int32, (CH, CH), 1)
    lane = lax.broadcasted_iota(jnp.int32, (CH, 2 * P_SIZE), 1)
    hidden = []
    for s in range(slots):
        ids = turned(rows_ref[s])[:, 3:4]
        visible = jnp.logical_and(ids == rows_ref[s, 3:4], position >= source)
        hidden.append(jnp.where(visible, 0.0, -1e30))
    scores = None
    for j in range(count):
        if j % (count // groups) == 0:
            g = j // (count // groups)
            scores = [
                lax.dot_general(
                    coupled_ref[s, :, g * 2 * N + N : (g + 1) * 2 * N],
                    coupled_ref[s, :, g * 2 * N : g * 2 * N + N],
                    (((1,), (1,)), ((), ())),
                    preferred_element_type=f32,
                )
                for s in range(slots)
            ]
        for s in range(slots):
            columns = turned(sums_ref[s, j])
            for pair in range(per_step // 2):
                mixing = []
                for h in (2 * pair, 2 * pair + 1):
                    damping = jnp.exp(
                        columns[:, h : h + 1] - sums_ref[s, j, h : h + 1] + hidden[s]
                    )
                    sizes = sums_ref[s, j, per_step + h : per_step + h + 1]
                    mixing.append((scores[s] * damping * sizes).astype(bf16))
                own = slice(j * WIDE + pair * 2 * P_SIZE, j * WIDE + (pair + 1) * 2 * P_SIZE)
                both = values_ref[s, :, own]
                mixed = dot(jnp.concatenate(mixing, axis=0), both)
                local_ref[s, :, own] = (
                    jnp.where(lane < P_SIZE, mixed[0:CH], mixed[CH : 2 * CH])
                    + per_head(skip_ref[...], j * per_step + 2 * pair, 2) * both.astype(f32)
                )
        own = slice(j * WIDE, (j + 1) * WIDE)
        projected = dot(rows, gate_ref[:, own]).astype(bf16)
        for s in range(slots):
            gates_ref[s, :, own] = projected[s * CH : (s + 1) * CH]


def unpacked(block):
    tail = block[block.shape[0] - FACTOR_ROWS :]
    return block[: block.shape[0] - FACTOR_ROWS], tail[0:1] + tail[1:2]


def paired(odd, mine_ref, got_ref):
    mine, got = mine_ref[...].astype(f32), got_ref[...].astype(f32)
    return unpacked(jnp.where(odd, got, mine)), unpacked(jnp.where(odd, mine, got))


def put_packed(out_ref, state, factor):
    lines = state.shape[0]
    out_ref[0:lines] = state.astype(bf16)
    if out_ref.shape[0] > lines:
        coarse = factor.astype(bf16).astype(f32)
        line = lax.broadcasted_iota(jnp.int32, (FACTOR_ROWS, state.shape[1]), 0)
        out_ref[lines : lines + FACTOR_ROWS] = jnp.where(
            line == 0, coarse, jnp.where(line == 1, factor - coarse, 0.0)
        ).astype(bf16)


def join_kernel(flags_ref, mine_ref, got_ref, out_ref):
    even, later = paired(flags_ref[0] == 1, mine_ref, got_ref)
    put_packed(out_ref, later[0] + later[1] * even[0], later[1] * even[1])


def chain_kernel(distance, flags_ref, mine_ref, got_ref, out_ref):
    state, factor = unpacked(mine_ref[...].astype(f32))
    earlier, leading = unpacked(got_ref[...].astype(f32))
    reached = jnp.where(flags_ref[2] >= distance, factor, 0.0)
    put_packed(out_ref, state + reached * earlier, reached * leading)


def entered(flags_ref, mine_ref, got_ref, before_ref):
    odd = flags_ref[0] == 1
    even, _ = paired(odd, mine_ref, got_ref)
    before = jnp.where(flags_ref[2] >= 2, before_ref[...].astype(f32), 0.0)
    between = even[0] + even[1] * before
    return jnp.where(odd, between, before), jnp.where(odd, before, between)


def finish_kernel(flags_ref, mine_ref, got_ref, before_ref, own_ref, other_ref):
    own, other = entered(flags_ref, mine_ref, got_ref, before_ref)
    own_ref[...] = own.astype(bf16)
    other_ref[...] = other.astype(bf16)


def out_kernel(slots, blocks, flags_ref, *refs):
    entry_refs, refs = refs[: 4 - slots], refs[4 - slots :]
    (
        local_ref,
        gates_ref,
        coupled_ref,
        sums_ref,
        rows_ref,
        gain_ref,
        out_ref,
        *refs,
    ) = refs
    pieces = 1 if slots == 2 else PIECES
    (
        first_ref,
        *second_refs,
        normed_scr,
    ) = refs[-(2 + pieces) :]
    wide = out_ref.shape[1] // blocks
    odd = flags_ref[0] == 1
    groups = coupled_ref.shape[2] // (2 * N)
    share = local_ref.shape[2] // groups
    count = sums_ref.shape[1]
    per_step = WIDE // P_SIZE
    if slots == 1:
        entries = [entered(flags_ref, *entry_refs)[0].astype(bf16)]
    else:
        own, other = [ref[...].astype(f32) for ref in entry_refs]
        entries = [jnp.where(odd, a, b).astype(bf16) for a, b in ((own, other), (other, own))]
    for s in range(slots):
        sums = jnp.concatenate([sums_ref[s, jj] for jj in range(count)], axis=0)
        line = lax.broadcasted_iota(jnp.int32, sums.shape, 0) % 8
        growth = rows_ref[s, 4:5] * jnp.exp(jnp.where(line < per_step, sums, 0.0))
        spread = spread_heads(turned(growth), per_step, count)
        for g in range(groups):
            own = slice(g * share, (g + 1) * share)
            queries = coupled_ref[s, :, g * 2 * N + N : (g + 1) * 2 * N]
            carried = dot(queries, entries[s][:, own])
            scanned = local_ref[s, :, own] + spread[:, own] * carried
            gated = scanned * jax.nn.silu(gates_ref[s, :, own].astype(f32))
            scale = lax.rsqrt(jnp.mean(gated * gated, axis=-1, keepdims=True) + epsilon)
            normed_scr[s * CH : (s + 1) * CH, own] = (gated * scale * gain_ref[:, own]).astype(
                bf16
            )

    normed = normed_scr[...]
    low = flags_ref[1] == 0
    for j in range(blocks):
        own = slice(j * wide, (j + 1) * wide)
        branch = dot(normed, out_ref[:, own])
        if slots == 2:
            first_ref[:, own] = branch[0:CH].astype(bf16)
            second_refs[0][:, own] = branch[CH : 2 * CH].astype(bf16)
        else:
            upper, lower = branch[0:HALF], branch[HALF:CH]
            first_ref[:, own] = jnp.where(low, upper, lower).astype(bf16)
            per_piece = blocks // len(second_refs)
            at = j % per_piece
            second_refs[j // per_piece][:, at * wide : (at + 1) * wide] = jnp.where(
                low, lower, upper
            ).astype(bf16)


def summed(refs):
    return sum(ref[...].astype(f32) for ref in refs)


def add_kernel(pieces, flags_ref, mine_ref, *refs):
    del flags_ref
    other_refs, out_ref = refs[:pieces], refs[-1]
    wide = out_ref.shape[1] // len(other_refs)
    for j, ref in enumerate(other_refs):
        own = slice(j * wide, (j + 1) * wide)
        out_ref[:, own] = (mine_ref[:, own].astype(f32) + ref[...].astype(f32)).astype(bf16)


def close_kernel(flags_ref, rezero_ref, own_ref, mine_ref, others_ref, *refs):
    *back, out_ref = refs
    chips, core = len(back) // 4, flags_ref[1]
    sums = [back[i * chips : (i + 1) * chips] for i in range(4)]
    ours = jnp.where(core == 0, summed(sums[0]), summed(sums[1]))
    theirs = jnp.where(core == 0, summed(sums[2]), summed(sums[3]))
    for at, far in ((core, ours), (1 - core, theirs)):
        lines = pl.ds(pl.multiple_of(at * HALF, HALF), HALF)
        branch = mine_ref[lines].astype(f32) + others_ref[lines].astype(f32) + far
        out_ref[lines] = (own_ref[lines].astype(f32) + rezero_ref[0] * branch).astype(bf16)


IN_VMEM = pl.BlockSpec(memory_space=pltpu.VMEM)
IN_SMEM = pl.BlockSpec(memory_space=pltpu.SMEM)
FLOPS_PER_US = 1_150_000_000


class Sequence:
    def __init__(self, flags):
        self.flags, self.token = flags, None

    def run(self, kernel, name, shapes, scratch, *operands, mib=2, us=1, scalars=()):
        tokens = [] if self.token is None else [self.token]
        given = 1 + len(scalars) + len(operands)

        def ordered(*refs):
            outs = refs[given + len(tokens) :]
            mark_ref = outs[len(shapes)]
            mark_ref[...] = jnp.zeros_like(mark_ref)
            kernel(*refs[:given], *outs[: len(shapes)], *outs[len(shapes) + 1 :])

        *results, self.token = pl.pallas_call(
            ordered,
            in_specs=[IN_SMEM] * (1 + len(scalars)) + [IN_VMEM] * (len(operands) + len(tokens)),
            out_specs=[IN_VMEM] * (len(shapes) + 1),
            out_shape=[*shapes, shape(f32, 8, CH)],
            scratch_shapes=scratch,
            compiler_params=pltpu.CompilerParams(vmem_limit_bytes=mib << 20),
            cost_estimate=pl.CostEstimate(
                flops=int(us * FLOPS_PER_US), bytes_accessed=0, transcendentals=0
            ),
            name=name,
        )(self.flags, *scalars, *operands, *tokens)
        return results

    def held(self, block):
        def hold(block_ref, token_ref, out_ref):
            del block_ref, token_ref, out_ref

        return pl.pallas_call(
            hold,
            in_specs=[IN_VMEM] * 2,
            out_specs=IN_VMEM,
            out_shape=shape(block.dtype, *block.shape),
            input_output_aliases={0: 0},
            compiler_params=pltpu.CompilerParams(vmem_limit_bytes=1 << 20),
            name="hold",
        )(block, self.token)


def shape(dtype, *sizes):
    return jax.ShapeDtypeStruct(sizes, dtype)


def mix(run, slots, streams, flip, sources, tails, segments, weights, small):
    value_weight, coupling_weight = weights
    width, narrow, depth = value_weight.shape[1], coupling_weight.shape[1], value_weight.shape[0]
    shapes = [
        shape(bf16, slots, CH, width),
        shape(bf16, slots, CH, narrow),
        shape(f32, slots, narrow // N, 8, CH),
        shape(f32, slots, 8, CH),
    ] + [shape(bf16, N + FACTOR_ROWS, width)] * slots
    scratch = [
        pltpu.VMEM((slots * CH + TAILS, depth), bf16),
        pltpu.VMEM((2, slots, CH + TAIL, WIDE), f32),
    ]
    kernel = functools.partial(mix_kernel, slots, streams, flip)
    operands = (*sources, *tails, segments, *weights, *small)
    return run(kernel, f"mix{slots}", shapes, scratch, *operands, mib=8, us=4 * slots)


def scan(run, slots, flip, sources, rows, gate_weight, values, coupled, sums, skip):
    shapes = [shape(bf16, *values.shape), shape(f32, *values.shape)]
    scratch = [pltpu.VMEM((slots * CH, gate_weight.shape[0]), bf16)]
    kernel = functools.partial(scan_kernel, slots, flip)
    operands = (*sources, rows, gate_weight, values, coupled, sums, skip)
    return run(kernel, f"scan{slots}", shapes, scratch, *operands, mib=6, us=0.1)


def project_out(run, slots, entries, local, gates, coupled, sums, rows, gain, out_weight, *waits):
    width, depth = out_weight.shape
    lines = CH if slots == 2 else HALF
    scratch = [pltpu.VMEM((slots * CH, width), bf16)]
    kernel = functools.partial(out_kernel, slots, 8)
    operands = (*entries, local, gates, coupled, sums, rows, gain, out_weight, *waits)
    pieces = 1 if slots == 2 else PIECES
    shapes = [shape(bf16, lines, depth)] + [shape(bf16, lines, depth // pieces)] * pieces
    return run(kernel, f"out{slots}", shapes, scratch, *operands, mib=6, us=0.1)


def along(block, distance):
    spans = lax.axis_size("ctx")
    return lax.ppermute(block, "ctx", [(i, (i + distance) % spans) for i in range(spans)])


def tail_from(block, chips_on):
    places, spans = lax.axis_size("fsdp"), lax.axis_size("ctx")
    route = [
        ((f + 2 * chips_on) % places * spans + c, f * spans + (c + 1) % spans)
        for f in range(places)
        for c in range(spans)
    ]
    return lax.ppermute(block, ("fsdp", "ctx"), route)


def partner(block, axis):
    return lax.ppermute(block, axis, [(i, i ^ 1) for i in range(lax.axis_size(axis))])


def over(block, distance):
    size = lax.axis_size("fsdp")
    return lax.ppermute(block, "fsdp", [(i, (i + 2 * distance) % size) for i in range(size)])


def joined(run, mine, got):
    return run(join_kernel, "join", [shape(bf16, *mine.shape)], [], mine, got, us=0.1)[0]


def chained(run, block):
    spans = lax.axis_size("ctx")
    lines, width = block.shape
    distance = 2
    while distance < spans // 2:
        last = 2 * distance >= spans // 2
        out = [shape(bf16, lines - FACTOR_ROWS if last else lines, width)]
        kernel = functools.partial(chain_kernel, distance)
        block = run(kernel, "chain", out, [], block, along(block, distance), us=0.1)[0]
        distance *= 2
    return block


def finished(run, kept, got, before):
    out = [shape(bf16, *before.shape)] * 2
    own, other = run(finish_kernel, "finish", out, [], kept, got, before, us=0.1)
    return own, partner(other, "ctx")


def on_device(
    tokens,
    segments,
    gate_weight,
    value_weight,
    coupling_weight,
    step_weight,
    value_conv,
    coupling_conv,
    value_shift,
    coupling_shift,
    step_bias,
    decay_log,
    skip_gain,
    norm_gain,
    out_weight,
    rezero,
):
    place = lax.axis_index("fsdp")
    span = lax.axis_index("ctx")
    chips = lax.axis_size("fsdp") // 2
    chip, core = place // 2, place % 2
    own = tokens[0]
    phases = [(d, j) for d in range(1, chips) for j in range(2)]
    far_streams = [(chip + d) % chips * 2 + j for d, j in phases]
    flags = jnp.stack([span % 2, core, span, place, place ^ 1] + far_streams).astype(jnp.int32)

    sequence = Sequence(flags)
    run = sequence.run

    arrived = {d: over(own, -d) for d in range(1, chips)}
    opposite = partner(own, "fsdp")
    half_shape = shape(bf16, HALF, own.shape[1])
    tail_shape = shape(bf16, TAILS, own.shape[1] // 2)
    tail = run(tail_kernel, "tail", [tail_shape], [], own, opposite, segments, us=8)[0]

    heads = step_weight.shape[1]
    head = jnp.broadcast_to(jnp.stack([step_bias, decay_log])[:, :, None], (2, heads, CH))
    skip = skip_gain[None]
    shifts = (value_shift[None], coupling_shift[None])
    small = (step_weight.T, value_conv, coupling_conv, *shifts, head)
    gain = norm_gain[None]

    weights = (value_weight, coupling_weight)
    near = tail_from(tail, 0)
    far = [tail_from(tail, d) for d in range(1, chips)]
    near_sources = (own, opposite)
    values, coupled, near_sums, near_rows, given, near_kept = mix(
        run, 2, (3, 4), None, near_sources, [near, *far], segments, weights, small
    )
    near_mixed = (values, coupled, near_sums)
    near_got = partner(given, "ctx")

    far_mixed = []
    for i, (d, j) in enumerate(phases):
        if j == 0:
            arrival = sequence.held(arrived[d])
            sources = (arrival, partner(arrival, "fsdp"))
        mixed = mix(
            run, 1, (5 + i,), j, sources, far[d - 1 : d], segments, weights, small
        )
        far_mixed.append((sources, *mixed, partner(mixed[-1], "ctx")))
        if i == 0:
            near_block = joined(run, near_kept, near_got)

    far_scans, blocks, befores = [], [], []
    for i, ((d, j), far_one) in enumerate(zip(phases, far_mixed)):
        sources, values, coupled, sums, rows, kept, got = far_one
        blocks.append(joined(run, kept, got))
        if i == 0:
            near_before = along(chained(run, near_block), 2)
        if i == 1:
            befores.append(along(chained(run, blocks[0]), 2))
        far_scans.append(
            scan(run, 1, j, sources, rows, gate_weight, values, coupled, sums, skip)
        )

    back, latest = {}, ()
    for i, ((d, j), (gates, local), far_one) in enumerate(zip(phases, far_scans, far_mixed)):
        _, _, coupled, sums, rows, kept, got = far_one
        mine, *pieces = project_out(
            run,
            1,
            (kept, got, befores[i]),
            local,
            gates,
            coupled,
            sums,
            rows,
            gain,
            out_weight,
            *(near_entries[1:] if i == 1 else ()),
        )
        pieces = [partner(piece, "fsdp") for piece in pieces]
        if i == 0:
            near_entries = finished(run, near_kept, near_got, near_before)
        kernel = functools.partial(add_kernel, len(pieces))
        total = run(kernel, "add", [half_shape], [], mine, *pieces, *latest, us=0.1)[0]
        back[d, j] = over(total, d)
        latest = (back[d, j],)
        if i == 0:
            befores += [along(chained(run, block), 2) for block in blocks[1:]]
            near_gates, near_local = scan(
                run, 2, None, near_sources, near_rows, gate_weight, *near_mixed, skip
            )

    near_mine, near_others = project_out(
        run,
        2,
        near_entries,
        near_local,
        near_gates,
        near_mixed[1],
        near_sums,
        near_rows,
        gain,
        out_weight,
    )
    near_others = partner(near_others, "fsdp")
    returned = [back[d, j] for j in range(2) for d in range(1, chips)]
    return run(
        close_kernel,
        "close",
        [shape(bf16, *own.shape)],
        [],
        own,
        near_mine,
        near_others,
        *returned,
        *[partner(block, "fsdp") for block in returned],
        mib=4,
        scalars=(rezero,),
    )[0][None]


def solution(mesh):
    return jax.shard_map(
        on_device,
        mesh=mesh,
        in_specs=(
            P("fsdp", "ctx", None),
            P(None, "ctx"),
            P(None, "fsdp"),
            P(None, "fsdp"),
            P(None, "fsdp"),
            P(None, "fsdp"),
            P(None, "fsdp"),
            P(None, "fsdp"),
            P("fsdp"),
            P("fsdp"),
            P("fsdp"),
            P("fsdp"),
            P("fsdp"),
            P("fsdp"),
            P("fsdp", None),
            P(),
        ),
        out_specs=P("fsdp", "ctx", None),
        check_vma=False,
    )
```

```python
import functools

import jax
import jax.numpy as jnp
from jax import lax
from jax.experimental import pallas as pl
from jax.experimental.pallas import tpu as pltpu
from jax.sharding import PartitionSpec as P

P_SIZE = 64
N = 128
CH = 128
HALF = CH // 2
TAIL = 8
TAILS = 16
WIDE = 256
PIECES = 2
FACTOR_ROWS = 16

epsilon = 1e-05
highest = lax.Precision.HIGHEST
f32 = jnp.float32
bf16 = jnp.bfloat16


def dot(a, b):
    return jnp.dot(a, b, preferred_element_type=f32)


def turned(rows):
    fill = jnp.zeros((N - rows.shape[0], rows.shape[1]), f32)
    return jnp.concatenate([rows, fill], axis=0).T


def per_head(columns, first, heads):
    lane = lax.broadcasted_iota(jnp.int32, (columns.shape[0], 2 * P_SIZE), 1)
    low = lane < P_SIZE
    blocks = [
        jnp.where(low, columns[:, c : c + 1], columns[:, c + 1 : c + 2])
        for c in range(first, first + heads, 2)
    ]
    return jnp.concatenate(blocks, axis=1)


def spread_heads(columns, heads_per_step, steps):
    return jnp.concatenate(
        [per_head(columns, 8 * j, heads_per_step) for j in range(steps)], axis=1
    )


def fill_rows(rows_scr, sources, core, flip):
    if flip is None:
        rows_scr[0:CH] = sources[0][...]
        rows_scr[CH : 2 * CH] = sources[1][...]
        return
    for ref, taken in zip(sources, (core == flip, core != flip)):

        @pl.when(taken)
        def _(ref=ref):
            rows_scr[0:CH] = ref[...]


def ids_row(flags_ref, segments_ref, at):
    ids = segments_ref[...].astype(f32)
    line = lax.broadcasted_iota(jnp.int32, ids.shape, 0)
    return jnp.sum(jnp.where(line == flags_ref[at], ids, 0.0), axis=0, keepdims=True)


def tail_kernel(flags_ref, own_ref, opposite_ref, segments_ref, tail_ref):
    half = tail_ref.shape[1]
    own, opposite = (
        ref[CH - TAILS : CH].astype(f32)[TAILS - TAIL :] for ref in (own_ref, opposite_ref)
    )
    line = lax.broadcasted_iota(jnp.int32, own.shape, 0)
    both = jnp.where(line < TAIL // 2, pltpu.roll(own, TAIL // 2, 0), opposite)
    line = line[:, 0:CH]
    labelled = jnp.where(
        line == 0,
        ids_row(flags_ref, segments_ref, 3),
        jnp.where(line == TAIL // 2, ids_row(flags_ref, segments_ref, 4), both[:, 0:CH]),
    )
    both = jnp.concatenate([labelled, both[:, CH:]], axis=1)
    tail_ref[...] = jnp.concatenate([both[:, :half], both[:, half:]]).astype(bf16)


def facts(rows_ref, s, ids, prior, reach):
    lane = lax.broadcasted_iota(jnp.int32, (8, CH), 1)
    line = lax.broadcasted_iota(jnp.int32, (8, CH), 0)
    ids, prior = (jnp.broadcast_to(a, (8, CH)) for a in (ids, prior))
    found = jnp.zeros((8, CH), f32)
    for k in range(reach):
        back = reach - k
        earlier = jnp.where(lane < back, pltpu.roll(prior, back, 1), pltpu.roll(ids, back, 1))
        found = jnp.where(line == k, jnp.where(earlier == ids, 1.0, 0.0), found)
    found = jnp.where(line == 3, ids, found)
    found = jnp.where(line == 4, jnp.where(ids == prior[:, CH - 1 : CH], 1.0, 0.0), found)
    found = jnp.where(line == 5, jnp.where(ids == ids[:, CH - 1 : CH], 1.0, 0.0), found)
    rows_ref[s] = found


def mix_kernel(slots, streams, flip, flags_ref, *refs):
    sources, refs = refs[:2], refs[2:]
    tail_ref, refs = refs[0], refs[-15 - slots :]
    segments_ref, value_ref, coupling_ref, step_ref, *taps_refs, head_ref = refs[:9]
    refs = refs[9:]
    values_ref, coupled_ref, sums_ref, rows_ref = refs[:4]
    state_refs, (rows_scr, pad_scr) = refs[4 : 4 + slots], refs[4 + slots :]
    odd = flags_ref[0] == 1
    heads = step_ref.shape[0]
    reach = 3
    count = sums_ref.shape[1]
    per_step = heads // count
    width = values_ref.shape[2]
    groups = coupled_ref.shape[2] // (2 * N)
    share = width // groups
    held = slots * CH

    work = []
    for g in range(groups):
        work.append((coupling_ref, coupled_ref, taps_refs[1::2], g))
        for piece in range(share // WIDE):
            work.append((value_ref, values_ref, taps_refs[0::2], g * (share // WIDE) + piece))
    fill_rows(rows_scr, sources, flags_ref[1], flip)
    later = flags_ref[2] > 0
    tail = jnp.where(later, tail_ref[...].astype(f32), 0.0)
    tail = jnp.concatenate([tail[0:TAIL], tail[TAIL:TAILS]], axis=1)
    tails = [pltpu.roll(tail, TAIL // 2, 0), tail]
    if slots == 1:
        tails = [jnp.where(flags_ref[1] == flip, *tails)] * 2
    rows_scr[held : held + TAILS] = jnp.concatenate(tails).astype(bf16)
    for s, tail in enumerate(tails[:slots]):
        facts(rows_ref, s, ids_row(flags_ref, segments_ref, streams[s]), tail[4:5, 0:CH], reach)
    masks = [turned(rows_ref[s]) for s in range(slots)]
    rows = rows_scr[...]
    step_rows = lax.dot_general(
        step_ref[...], rows_scr[0:held], (((1,), (1,)), ((), ())), preferred_element_type=f32
    )

    def convolved(projected, out_ref, taps_and_shift, at, slot):
        projected = projected.astype(bf16).astype(f32)
        taps, shift = (ref[:, at * WIDE : (at + 1) * WIDE].astype(f32) for ref in taps_and_shift)
        for s in range(slots):
            body = projected[CH * s : CH * (s + 1)]
            start = held + TAIL * s
            pad_scr[slot, s, 0:TAIL] = projected[start : start + TAIL]
            pad_scr[slot, s, TAIL : TAIL + CH] = body
            running = shift + taps[reach : reach + 1] * body
            for k in range(reach):
                window = pad_scr[slot, s, TAIL - reach + k : TAIL - reach + k + CH]
                running = running + taps[k : k + 1] * window * masks[s][:, k : k + 1]
            out_ref[s, :, at * WIDE : (at + 1) * WIDE] = jax.nn.silu(running).astype(bf16)

    source = lax.broadcasted_iota(jnp.int32, (CH, CH), 0)
    position = lax.broadcasted_iota(jnp.int32, (CH, CH), 1)
    upto = (source <= position).astype(f32)

    def put_states(parts, first, columns):
        if slots == 1:
            state_refs[0][first : first + parts[0].shape[0], columns] = parts[0].astype(bf16)
            return
        given = jnp.where(odd, parts[1], parts[0]).astype(bf16)
        kept = jnp.where(odd, parts[0], parts[1]).astype(bf16)
        for ref, part in zip(state_refs, (given, kept)):
            ref[first : first + part.shape[0], columns] = part

    def weighed(s):
        sizes = jax.nn.softplus(
            step_rows[:, s * CH : (s + 1) * CH].astype(bf16).astype(f32) + head_ref[0]
        )
        decays = -sizes * jnp.exp(head_ref[1])
        cumulative = jnp.dot(decays, upto, precision=highest, preferred_element_type=f32)
        last = cumulative[:, CH - 1 : CH]
        kept, ending = rows_ref[s, 4:5], rows_ref[s, 5:6]
        tail_weight = ending * jnp.exp(last - cumulative) * sizes
        growth = kept * jnp.exp(cumulative)
        gap = jnp.zeros((8 - per_step, CH), f32)
        spaced_tail, spaced_growth = [], []
        for jj in range(count):
            own = slice(jj * per_step, (jj + 1) * per_step)
            sums_ref[s, jj, 0:per_step] = cumulative[own]
            sums_ref[s, jj, per_step : 2 * per_step] = sizes[own]
            spaced_tail += [tail_weight[own], gap]
            spaced_growth += [growth[own], gap]
        leading = spread_heads(
            turned(jnp.concatenate(spaced_growth, axis=0))[CH - 8 : CH], per_step, count
        )[7:8]
        coarse = leading.astype(bf16).astype(f32)
        line = lax.broadcasted_iota(jnp.int32, (FACTOR_ROWS, width), 0)
        factor = jnp.where(line == 0, coarse, jnp.where(line == 1, leading - coarse, 0.0))
        return turned(jnp.concatenate(spaced_tail, axis=0)), factor

    def ended(g):
        own = slice(g * share, (g + 1) * share)
        parts = []
        for s in range(slots):
            part = spread_heads(
                weights[s][0][:, g * 8 * count // groups : (g + 1) * 8 * count // groups],
                per_step,
                count // groups,
            )
            weighted = (part * values_ref[s, :, own].astype(f32)).astype(bf16)
            keys = coupled_ref[s, :, g * 2 * N : g * 2 * N + N]
            parts.append(
                lax.dot_general(
                    keys, weighted, (((0,), (0,)), ((), ())), preferred_element_type=f32
                )
            )
        put_states(parts, 0, own)

    weights = [weighed(s) for s in range(slots)]
    put_states([w[1] for w in weights], N, slice(0, width))
    per_group = len(work) // groups
    waiting = None
    for i in range(len(work) + 1):
        following = None
        if i < len(work):
            weight_ref, out_ref, taps_and_shift, at = work[i]
            following = (
                dot(rows, weight_ref[:, at * WIDE : (at + 1) * WIDE]),
                out_ref,
                taps_and_shift,
                at,
                i % 2,
            )
        if waiting is not None:
            convolved(*waiting)
            if i % per_group == 0:
                ended(i // per_group - 1)
        waiting = following


def scan_kernel(slots, flip, flags_ref, *refs):
    sources, refs = refs[:2], refs[2:]
    (
        rows_ref,
        gate_ref,
        values_ref,
        coupled_ref,
        sums_ref,
        skip_ref,
        gates_ref,
        local_ref,
        rows_scr,
    ) = refs
    count = sums_ref.shape[1]
    groups = coupled_ref.shape[2] // (2 * N)
    per_step = WIDE // P_SIZE
    fill_rows(rows_scr, sources, flags_ref[1], flip)
    rows = rows_scr[...]
    position = lax.broadcasted_iota(jnp.int32, (CH, CH), 0)
    source = lax.broadcasted_iota(jnp.int32, (CH, CH), 1)
    lane = lax.broadcasted_iota(jnp.int32, (CH, 2 * P_SIZE), 1)
    hidden = []
    for s in range(slots):
        ids = turned(rows_ref[s])[:, 3:4]
        visible = jnp.logical_and(ids == rows_ref[s, 3:4], position >= source)
        hidden.append(jnp.where(visible, 0.0, -1e30))
    scores = None
    for j in range(count):
        if j % (count // groups) == 0:
            g = j // (count // groups)
            scores = [
                lax.dot_general(
                    coupled_ref[s, :, g * 2 * N + N : (g + 1) * 2 * N],
                    coupled_ref[s, :, g * 2 * N : g * 2 * N + N],
                    (((1,), (1,)), ((), ())),
                    preferred_element_type=f32,
                )
                for s in range(slots)
            ]
        for s in range(slots):
            columns = turned(sums_ref[s, j])
            for pair in range(per_step // 2):
                mixing = []
                for h in (2 * pair, 2 * pair + 1):
                    damping = jnp.exp(
                        columns[:, h : h + 1] - sums_ref[s, j, h : h + 1] + hidden[s]
                    )
                    sizes = sums_ref[s, j, per_step + h : per_step + h + 1]
                    mixing.append((scores[s] * damping * sizes).astype(bf16))
                own = slice(j * WIDE + pair * 2 * P_SIZE, j * WIDE + (pair + 1) * 2 * P_SIZE)
                both = values_ref[s, :, own]
                mixed = dot(jnp.concatenate(mixing, axis=0), both)
                local_ref[s, :, own] = (
                    jnp.where(lane < P_SIZE, mixed[0:CH], mixed[CH : 2 * CH])
                    + per_head(skip_ref[...], j * per_step + 2 * pair, 2) * both.astype(f32)
                )
        own = slice(j * WIDE, (j + 1) * WIDE)
        projected = dot(rows, gate_ref[:, own]).astype(bf16)
        for s in range(slots):
            gates_ref[s, :, own] = projected[s * CH : (s + 1) * CH]


def unpacked(block):
    tail = block[block.shape[0] - FACTOR_ROWS :]
    return block[: block.shape[0] - FACTOR_ROWS], tail[0:1] + tail[1:2]


def paired(odd, mine_ref, got_ref):
    mine, got = mine_ref[...].astype(f32), got_ref[...].astype(f32)
    return unpacked(jnp.where(odd, got, mine)), unpacked(jnp.where(odd, mine, got))


def put_packed(out_ref, state, factor):
    lines = state.shape[0]
    out_ref[0:lines] = state.astype(bf16)
    if out_ref.shape[0] > lines:
        coarse = factor.astype(bf16).astype(f32)
        line = lax.broadcasted_iota(jnp.int32, (FACTOR_ROWS, state.shape[1]), 0)
        out_ref[lines : lines + FACTOR_ROWS] = jnp.where(
            line == 0, coarse, jnp.where(line == 1, factor - coarse, 0.0)
        ).astype(bf16)


def join_kernel(flags_ref, mine_ref, got_ref, out_ref):
    even, later = paired(flags_ref[0] == 1, mine_ref, got_ref)
    put_packed(out_ref, later[0] + later[1] * even[0], later[1] * even[1])


def chain_kernel(distance, flags_ref, mine_ref, got_ref, out_ref):
    state, factor = unpacked(mine_ref[...].astype(f32))
    earlier, leading = unpacked(got_ref[...].astype(f32))
    reached = jnp.where(flags_ref[2] >= distance, factor, 0.0)
    put_packed(out_ref, state + reached * earlier, reached * leading)


def entered(flags_ref, mine_ref, got_ref, before_ref):
    odd = flags_ref[0] == 1
    even, _ = paired(odd, mine_ref, got_ref)
    before = jnp.where(flags_ref[2] >= 2, before_ref[...].astype(f32), 0.0)
    between = even[0] + even[1] * before
    return jnp.where(odd, between, before), jnp.where(odd, before, between)


def finish_kernel(flags_ref, mine_ref, got_ref, before_ref, own_ref, other_ref):
    own, other = entered(flags_ref, mine_ref, got_ref, before_ref)
    own_ref[...] = own.astype(bf16)
    other_ref[...] = other.astype(bf16)


def out_kernel(slots, blocks, flags_ref, *refs):
    entry_refs, refs = refs[: 4 - slots], refs[4 - slots :]
    (
        local_ref,
        gates_ref,
        coupled_ref,
        sums_ref,
        rows_ref,
        gain_ref,
        out_ref,
        *refs,
    ) = refs
    pieces = 1 if slots == 2 else PIECES
    (
        first_ref,
        *second_refs,
        normed_scr,
    ) = refs[-(2 + pieces) :]
    wide = out_ref.shape[1] // blocks
    odd = flags_ref[0] == 1
    groups = coupled_ref.shape[2] // (2 * N)
    share = local_ref.shape[2] // groups
    count = sums_ref.shape[1]
    per_step = WIDE // P_SIZE
    if slots == 1:
        entries = [entered(flags_ref, *entry_refs)[0].astype(bf16)]
    else:
        own, other = [ref[...].astype(f32) for ref in entry_refs]
        entries = [jnp.where(odd, a, b).astype(bf16) for a, b in ((own, other), (other, own))]
    for s in range(slots):
        sums = jnp.concatenate([sums_ref[s, jj] for jj in range(count)], axis=0)
        line = lax.broadcasted_iota(jnp.int32, sums.shape, 0) % 8
        growth = rows_ref[s, 4:5] * jnp.exp(jnp.where(line < per_step, sums, 0.0))
        spread = spread_heads(turned(growth), per_step, count)
        for g in range(groups):
            own = slice(g * share, (g + 1) * share)
            queries = coupled_ref[s, :, g * 2 * N + N : (g + 1) * 2 * N]
            carried = dot(queries, entries[s][:, own])
            scanned = local_ref[s, :, own] + spread[:, own] * carried
            gated = scanned * jax.nn.silu(gates_ref[s, :, own].astype(f32))
            scale = lax.rsqrt(jnp.mean(gated * gated, axis=-1, keepdims=True) + epsilon)
            normed_scr[s * CH : (s + 1) * CH, own] = (gated * scale * gain_ref[:, own]).astype(
                bf16
            )

    normed = normed_scr[...]
    low = flags_ref[1] == 0
    for j in range(blocks):
        own = slice(j * wide, (j + 1) * wide)
        branch = dot(normed, out_ref[:, own])
        if slots == 2:
            first_ref[:, own] = branch[0:CH].astype(bf16)
            second_refs[0][:, own] = branch[CH : 2 * CH].astype(bf16)
        else:
            upper, lower = branch[0:HALF], branch[HALF:CH]
            first_ref[:, own] = jnp.where(low, upper, lower).astype(bf16)
            per_piece = blocks // len(second_refs)
            at = j % per_piece
            second_refs[j // per_piece][:, at * wide : (at + 1) * wide] = jnp.where(
                low, lower, upper
            ).astype(bf16)


def summed(refs):
    return sum(ref[...].astype(f32) for ref in refs)


def add_kernel(pieces, flags_ref, mine_ref, *refs):
    del flags_ref
    other_refs, out_ref = refs[:pieces], refs[-1]
    wide = out_ref.shape[1] // len(other_refs)
    for j, ref in enumerate(other_refs):
        own = slice(j * wide, (j + 1) * wide)
        out_ref[:, own] = (mine_ref[:, own].astype(f32) + ref[...].astype(f32)).astype(bf16)


def close_kernel(flags_ref, rezero_ref, own_ref, mine_ref, others_ref, *refs):
    *back, out_ref = refs
    chips, core = len(back) // 4, flags_ref[1]
    sums = [back[i * chips : (i + 1) * chips] for i in range(4)]
    ours = jnp.where(core == 0, summed(sums[0]), summed(sums[1]))
    theirs = jnp.where(core == 0, summed(sums[2]), summed(sums[3]))
    for at, far in ((core, ours), (1 - core, theirs)):
        lines = pl.ds(pl.multiple_of(at * HALF, HALF), HALF)
        branch = mine_ref[lines].astype(f32) + others_ref[lines].astype(f32) + far
        out_ref[lines] = (own_ref[lines].astype(f32) + rezero_ref[0] * branch).astype(bf16)


IN_VMEM = pl.BlockSpec(memory_space=pltpu.VMEM)
IN_SMEM = pl.BlockSpec(memory_space=pltpu.SMEM)
FLOPS_PER_US = 1_150_000_000


class Sequence:
    def __init__(self, flags):
        self.flags, self.token = flags, None

    def run(self, kernel, name, shapes, scratch, *operands, mib=2, us=1, scalars=()):
        tokens = [] if self.token is None else [self.token]
        given = 1 + len(scalars) + len(operands)

        def ordered(*refs):
            outs = refs[given + len(tokens) :]
            mark_ref = outs[len(shapes)]
            mark_ref[...] = jnp.zeros_like(mark_ref)
            kernel(*refs[:given], *outs[: len(shapes)], *outs[len(shapes) + 1 :])

        *results, self.token = pl.pallas_call(
            ordered,
            in_specs=[IN_SMEM] * (1 + len(scalars)) + [IN_VMEM] * (len(operands) + len(tokens)),
            out_specs=[IN_VMEM] * (len(shapes) + 1),
            out_shape=[*shapes, shape(f32, 8, CH)],
            scratch_shapes=scratch,
            compiler_params=pltpu.CompilerParams(vmem_limit_bytes=mib << 20),
            cost_estimate=pl.CostEstimate(
                flops=int(us * FLOPS_PER_US), bytes_accessed=0, transcendentals=0
            ),
            name=name,
        )(self.flags, *scalars, *operands, *tokens)
        return results

    def held(self, block):
        def hold(block_ref, token_ref, out_ref):
            del block_ref, token_ref, out_ref

        return pl.pallas_call(
            hold,
            in_specs=[IN_VMEM] * 2,
            out_specs=IN_VMEM,
            out_shape=shape(block.dtype, *block.shape),
            input_output_aliases={0: 0},
            compiler_params=pltpu.CompilerParams(vmem_limit_bytes=1 << 20),
            name="hold",
        )(block, self.token)


def shape(dtype, *sizes):
    return jax.ShapeDtypeStruct(sizes, dtype)


def mix(run, slots, streams, flip, sources, tails, segments, weights, small):
    value_weight, coupling_weight = weights
    width, narrow, depth = value_weight.shape[1], coupling_weight.shape[1], value_weight.shape[0]
    shapes = [
        shape(bf16, slots, CH, width),
        shape(bf16, slots, CH, narrow),
        shape(f32, slots, narrow // N, 8, CH),
        shape(f32, slots, 8, CH),
    ] + [shape(bf16, N + FACTOR_ROWS, width)] * slots
    scratch = [
        pltpu.VMEM((slots * CH + TAILS, depth), bf16),
        pltpu.VMEM((2, slots, CH + TAIL, WIDE), f32),
    ]
    kernel = functools.partial(mix_kernel, slots, streams, flip)
    operands = (*sources, *tails, segments, *weights, *small)
    return run(kernel, f"mix{slots}", shapes, scratch, *operands, mib=8, us=4 * slots)


def scan(run, slots, flip, sources, rows, gate_weight, values, coupled, sums, skip):
    shapes = [shape(bf16, *values.shape), shape(f32, *values.shape)]
    scratch = [pltpu.VMEM((slots * CH, gate_weight.shape[0]), bf16)]
    kernel = functools.partial(scan_kernel, slots, flip)
    operands = (*sources, rows, gate_weight, values, coupled, sums, skip)
    return run(kernel, f"scan{slots}", shapes, scratch, *operands, mib=6, us=0.1)


def project_out(run, slots, entries, local, gates, coupled, sums, rows, gain, out_weight, *waits):
    width, depth = out_weight.shape
    lines = CH if slots == 2 else HALF
    scratch = [pltpu.VMEM((slots * CH, width), bf16)]
    kernel = functools.partial(out_kernel, slots, 4)
    operands = (*entries, local, gates, coupled, sums, rows, gain, out_weight, *waits)
    pieces = 1 if slots == 2 else PIECES
    shapes = [shape(bf16, lines, depth)] + [shape(bf16, lines, depth // pieces)] * pieces
    return run(kernel, f"out{slots}", shapes, scratch, *operands, mib=6, us=0.1)


def along(block, distance):
    spans = lax.axis_size("ctx")
    return lax.ppermute(block, "ctx", [(i, (i + distance) % spans) for i in range(spans)])


def tail_from(block, chips_on):
    places, spans = lax.axis_size("fsdp"), lax.axis_size("ctx")
    route = [
        ((f + 2 * chips_on) % places * spans + c, f * spans + (c + 1) % spans)
        for f in range(places)
        for c in range(spans)
    ]
    return lax.ppermute(block, ("fsdp", "ctx"), route)


def partner(block, axis):
    return lax.ppermute(block, axis, [(i, i ^ 1) for i in range(lax.axis_size(axis))])


def over(block, distance):
    size = lax.axis_size("fsdp")
    return lax.ppermute(block, "fsdp", [(i, (i + 2 * distance) % size) for i in range(size)])


def joined(run, mine, got):
    return run(join_kernel, "join", [shape(bf16, *mine.shape)], [], mine, got, us=0.1)[0]


def chained(run, block):
    spans = lax.axis_size("ctx")
    lines, width = block.shape
    distance = 2
    while distance < spans // 2:
        last = 2 * distance >= spans // 2
        out = [shape(bf16, lines - FACTOR_ROWS if last else lines, width)]
        kernel = functools.partial(chain_kernel, distance)
        block = run(kernel, "chain", out, [], block, along(block, distance), us=0.1)[0]
        distance *= 2
    return block


def finished(run, kept, got, before):
    out = [shape(bf16, *before.shape)] * 2
    own, other = run(finish_kernel, "finish", out, [], kept, got, before, us=0.1)
    return own, partner(other, "ctx")


def on_device(
    tokens,
    segments,
    gate_weight,
    value_weight,
    coupling_weight,
    step_weight,
    value_conv,
    coupling_conv,
    value_shift,
    coupling_shift,
    step_bias,
    decay_log,
    skip_gain,
    norm_gain,
    out_weight,
    rezero,
):
    place = lax.axis_index("fsdp")
    span = lax.axis_index("ctx")
    chips = lax.axis_size("fsdp") // 2
    chip, core = place // 2, place % 2
    own = tokens[0]
    phases = [(d, j) for d in range(1, chips) for j in range(2)]
    far_streams = [(chip + d) % chips * 2 + j for d, j in phases]
    flags = jnp.stack([span % 2, core, span, place, place ^ 1] + far_streams).astype(jnp.int32)

    sequence = Sequence(flags)
    run = sequence.run

    arrived = {d: over(own, -d) for d in range(1, chips)}
    opposite = partner(own, "fsdp")
    half_shape = shape(bf16, HALF, own.shape[1])
    tail_shape = shape(bf16, TAILS, own.shape[1] // 2)
    tail = run(tail_kernel, "tail", [tail_shape], [], own, opposite, segments, us=8)[0]

    heads = step_weight.shape[1]
    head = jnp.broadcast_to(jnp.stack([step_bias, decay_log])[:, :, None], (2, heads, CH))
    skip = skip_gain[None]
    shifts = (value_shift[None], coupling_shift[None])
    small = (step_weight.T, value_conv, coupling_conv, *shifts, head)
    gain = norm_gain[None]

    weights = (value_weight, coupling_weight)
    near = tail_from(tail, 0)
    far = [tail_from(tail, d) for d in range(1, chips)]
    near_sources = (own, opposite)
    values, coupled, near_sums, near_rows, given, near_kept = mix(
        run, 2, (3, 4), None, near_sources, [near, *far], segments, weights, small
    )
    near_mixed = (values, coupled, near_sums)
    near_got = partner(given, "ctx")

    far_mixed = []
    for i, (d, j) in enumerate(phases):
        if j == 0:
            arrival = sequence.held(arrived[d])
            sources = (arrival, partner(arrival, "fsdp"))
        mixed = mix(
            run, 1, (5 + i,), j, sources, far[d - 1 : d], segments, weights, small
        )
        far_mixed.append((sources, *mixed, partner(mixed[-1], "ctx")))
        if i == 0:
            near_block = joined(run, near_kept, near_got)

    far_scans, blocks, befores = [], [], []
    for i, ((d, j), far_one) in enumerate(zip(phases, far_mixed)):
        sources, values, coupled, sums, rows, kept, got = far_one
        blocks.append(joined(run, kept, got))
        if i == 0:
            near_before = along(chained(run, near_block), 2)
        if i == 1:
            befores.append(along(chained(run, blocks[0]), 2))
        far_scans.append(
            scan(run, 1, j, sources, rows, gate_weight, values, coupled, sums, skip)
        )

    back, latest = {}, ()
    for i, ((d, j), (gates, local), far_one) in enumerate(zip(phases, far_scans, far_mixed)):
        _, _, coupled, sums, rows, kept, got = far_one
        mine, *pieces = project_out(
            run,
            1,
            (kept, got, befores[i]),
            local,
            gates,
            coupled,
            sums,
            rows,
            gain,
            out_weight,
            *(near_entries[1:] if i == 1 else ()),
        )
        pieces = [partner(piece, "fsdp") for piece in pieces]
        if i == 0:
            near_entries = finished(run, near_kept, near_got, near_before)
        kernel = functools.partial(add_kernel, len(pieces))
        total = run(kernel, "add", [half_shape], [], mine, *pieces, *latest, us=0.1)[0]
        back[d, j] = over(total, d)
        latest = (back[d, j],)
        if i == 0:
            befores += [along(chained(run, block), 2) for block in blocks[1:]]
            near_gates, near_local = scan(
                run, 2, None, near_sources, near_rows, gate_weight, *near_mixed, skip
            )

    near_mine, near_others = project_out(
        run,
        2,
        near_entries,
        near_local,
        near_gates,
        near_mixed[1],
        near_sums,
        near_rows,
        gain,
        out_weight,
    )
    near_others = partner(near_others, "fsdp")
    returned = [back[d, j] for j in range(2) for d in range(1, chips)]
    return run(
        close_kernel,
        "close",
        [shape(bf16, *own.shape)],
        [],
        own,
        near_mine,
        near_others,
        *returned,
        *[partner(block, "fsdp") for block in returned],
        mib=4,
        scalars=(rezero,),
    )[0][None]


def solution(mesh):
    return jax.shard_map(
        on_device,
        mesh=mesh,
        in_specs=(
            P("fsdp", "ctx", None),
            P(None, "ctx"),
            P(None, "fsdp"),
            P(None, "fsdp"),
            P(None, "fsdp"),
            P(None, "fsdp"),
            P(None, "fsdp"),
            P(None, "fsdp"),
            P("fsdp"),
            P("fsdp"),
            P("fsdp"),
            P("fsdp"),
            P("fsdp"),
            P("fsdp"),
            P("fsdp", None),
            P(),
        ),
        out_specs=P("fsdp", "ctx", None),
        check_vma=False,
    )
```
